32 devices in a mesh: energy: 2 (over y), trans: 8 (over z, x), cross: 2 (over core).
Axes of the slice: x: 2, y: 2, z: 4, core: 2. Of those that a mesh axis runs over, the one named last changes fastest.
Arguments:
- sources: float32 [64, 8, 64, 128], P(('energy', 'trans'), 'cross'), parts along dimension 0, may hold values from -6 to 6
- couplings: float32 [64, 8, 7, 64, 64], P(('energy', 'trans'), 'cross'), parts along dimension 0
- block_cols: int32 [32, 8, 7], P('trans', 'cross'), may hold values from 0 to 23, as said below
- lead_sites: int32 [4], replicated, may hold values from 0 to 7, as said below
- lead_sigma: float32 [8, 64, 64], P('energy'), parts along dimension 0
Outputs:
- basis: bfloat16 [64, 8, 64, 512], P(('energy', 'trans'), 'cross'), parts along dimension 0
- r_factor: float32 [1024, 512], P('energy'), parts along dimension 0
The draws below stay inside these ranges and needn't reach their ends.
There are 2 independent parts, one for each index of `energy`. The reference program is written for one: setup_inputs(seed, part) draws one part's arguments, and reference() takes and returns one part's arrays. A program takes and returns all parts, laid end to end along the dimension named above; an argument that names none is the same for every part. Nothing has to cross between parts.
Inputs may be any that keep to these rules, and one draw needn't show every extreme that they name: `block_cols`: slot 0 of every block row names the row's own block, 8 plus its cross position; an entry c names the block at cross position c % 8 in the layer c // 8 - 1 steps away, which is absent beyond the wire's ends. `lead_sites`: the first 2 entries are the contacts at layer 0, the last 2 those at layer 31; the positions of one end are distinct.
All inputs are finite; a program needn't handle non-finite values.
Results may differ from the reference program's by a relative error of at most 0.001.
Values sent between devices are 32-bit elements; how exact they have to be, the bound alone decides.
No kernel may reach another device: no remote copies, remote signals or barrier semaphores. Data moves between devices by JAX's collectives and lax.ppermute only.
A program may use at most 64 MiB of HBM per device.

```python
import math
import jax
import jax.numpy as jnp
from jax import lax

B = 64
R = 128
S = 3
NNZ = 7
NCONT = 2
NL = 32
NCB = 8
NROWS = 16384


def draw_couplings(key, part):
    key = jax.random.fold_in(key, 11)
    key_coupling, key_diagonal = jax.random.split(key)
    spread = 0.5 / math.sqrt(NNZ * B)
    coupling = jax.random.truncated_normal(key_coupling, -4.0, 4.0, (NL, NCB, NNZ, B, B), jnp.float32) * spread
    diagonal = jax.random.uniform(key_diagonal, (NL, NCB, B), jnp.float32, 1.0, 3.0)
    identity = jnp.eye(B, dtype=jnp.float32)
    leading = (jnp.arange(NNZ) == 0).astype(jnp.float32)[None, None, :, None, None]
    return coupling + leading * diagonal[:, :, None, :, None] * identity


def draw_block_cols(key, part):
    key = jax.random.fold_in(key, 12)
    key_layer, key_cross = jax.random.split(key)
    offsets = jax.random.randint(key_layer, (NL, NCB, NNZ), 0, 3)
    across = jax.random.randint(key_cross, (NL, NCB, NNZ), 0, NCB)
    chosen = offsets * NCB + across
    own_block = NCB + jnp.arange(NCB, dtype=jnp.int32)
    slots = jnp.arange(NNZ, dtype=jnp.int32)[None, None, :]
    return jnp.where(slots == 0, own_block[None, :, None], chosen).astype(jnp.int32)


def draw_lead_sites(key, part):
    key = jax.random.fold_in(key, 13)
    key_left, key_right = jax.random.split(key)
    order_left = jax.random.permutation(key_left, NCB)
    order_right = jax.random.permutation(key_right, NCB)
    left_sites = (order_left[:NCONT] - order_left[0]) % NCB
    right_sites = (order_right[:NCONT] - order_right[0] + NCB - 1) % NCB
    return jnp.concatenate([left_sites, right_sites]).astype(jnp.int32)


def draw_lead_sigma(key, part):
    key = jax.random.fold_in(key, 14)
    spread = 0.5 / math.sqrt(B)
    values = jax.random.truncated_normal(key, -4.0, 4.0, (2 * NCONT, B, B), jnp.float32) * spread
    return values


def steps_of(key, dims, pieces, least, top_value):
    def one(position, blocks):
        steps = jax.random.uniform(jax.random.fold_in(jax.random.fold_in(key, 6), position), (blocks,), jnp.float32, least / len(pieces), top_value / len(pieces))
        return jnp.repeat(jnp.exp(steps), dims[position] // blocks).reshape((-1,) + (1,) * (len(dims) - position - 1))

    loudness = one(*pieces[0])
    for cut in pieces[1:]:
        loudness = loudness * one(*cut)
    return loudness


def centred(stream_key, dims, scale, bound, pieces=(), held_as=jnp.bfloat16):
    loudness = steps_of(stream_key, dims, pieces, -0.22, 0.18) if pieces else 1.0
    drawn = jax.random.normal(stream_key, dims, jnp.float32) * scale * loudness
    return jnp.minimum(jnp.maximum(drawn, -bound), bound).astype(held_as)


def setup_inputs(seed: int = 0, part: int = 0) -> dict:
    keys = jax.random.split(jax.random.key(seed), 6)
    own_keys = jax.random.split(jax.random.fold_in(keys[5], part), 6)
    return {
        "sources": centred(own_keys[0], (NL, NCB, B, R), 1.0, 6.0, ((0, 8), (1, 2)), jnp.float32),
        "couplings": draw_couplings(jax.random.fold_in(jax.random.fold_in(keys[5], part), 71), part),
        "block_cols": draw_block_cols(jax.random.fold_in(keys[5], 71), part),
        "lead_sites": draw_lead_sites(jax.random.fold_in(keys[5], 71), part),
        "lead_sigma": draw_lead_sigma(jax.random.fold_in(jax.random.fold_in(keys[5], part), 71), part),
    }


center_shift = 2.0
half_range = 1.6

def lead_blocks(lead_sites, lead_sigma, positions):
    count = lead_sites.shape[0] // 2
    match = (lead_sites[:, None] == positions[None, :]).astype(jnp.float32)
    left_side = (jnp.arange(2 * count, dtype=jnp.int32) < count).astype(jnp.float32)[:, None]
    first_term = jnp.einsum('kc,kab->cab', match * left_side, lead_sigma, precision=lax.Precision.HIGHEST)
    last_term = jnp.einsum('kc,kab->cab', match * (1.0 - left_side), lead_sigma, precision=lax.Precision.HIGHEST)
    return (first_term, last_term)

def reference(sources, couplings, block_cols, lead_sites, lead_sigma):
    first_term, last_term = lead_blocks(lead_sites, lead_sigma, jnp.arange(NCB, dtype=jnp.int32))

    def operate(field):
        padded = jnp.pad(field, ((1, 1), (0, 0), (0, 0), (0, 0)))
        flat = padded.reshape(-1, B, R)

        def one_layer(layer):
            picked = flat[layer * NCB + block_cols[layer]]
            return jnp.einsum('cjab,cjbr->car', couplings[layer], picked, precision=lax.Precision.HIGHEST)
        result = lax.map(one_layer, jnp.arange(NL, dtype=jnp.int32))
        result = result.at[0].add(-jnp.einsum('cab,cbr->car', first_term, field[0], precision=lax.Precision.HIGHEST))
        result = result.at[NL - 1].add(-jnp.einsum('cab,cbr->car', last_term, field[NL - 1], precision=lax.Precision.HIGHEST))
        return result
    powers = [sources]
    current = (operate(sources) - center_shift * sources) / half_range
    powers.append(current)
    for step in range(S - 1):
        following = 2.0 * (operate(powers[-1]) - center_shift * powers[-1]) / half_range - powers[-2]
        powers.append(following)
    total_cols = (S + 1) * R
    krylov = jnp.concatenate(powers, axis=-1).reshape(NROWS, total_cols)
    gram = lax.dot_general(krylov, krylov, (((0,), (0,)), ((), ())), precision=lax.Precision.HIGHEST)
    lower = jnp.linalg.cholesky(gram)
    solved = jax.scipy.linalg.solve_triangular(lower, krylov.T, lower=True)
    scale_rows = math.sqrt(NROWS)
    basis = (solved.T * scale_rows).astype(jnp.bfloat16).reshape(NL, NCB, B, total_cols)
    return (basis, lower.T / scale_rows)
```

```python
import functools
import math

import jax
import jax.numpy as jnp
from jax import lax
from jax.experimental import pallas as pl
from jax.experimental.pallas import tpu as pltpu
from jax.sharding import PartitionSpec as P

S = 3
center_shift = 2.0
half_range = 1.6
HIGH = lax.Precision.HIGH
HIGHEST = lax.Precision.HIGHEST
VMEM_LIMIT = 48 * 1024 * 1024


def split(x):
    high = x.astype(jnp.bfloat16)
    low = (x - high.astype(jnp.float32)).astype(jnp.bfloat16)
    return high, low


def pack_kernel(count, cross_local, layers, slots, info, sites, couplings, sigma, out):
    layer = pl.program_id(0)
    first = jnp.logical_and(layer == 0, info[1] == 1)
    last = jnp.logical_and(layer == layers - 1, info[2] == 1)
    for q in range(cross_local):
        place = info[0] * cross_local + q
        lead = None
        for k in range(2 * count):
            flag = first if k < count else last
            weight = jnp.where(jnp.logical_and(flag, sites[k] == place), -1.0, 0.0)
            term = sigma[k] * weight
            lead = term if lead is None else lead + term
        blocks = [couplings[0, q, j] for j in range(slots)] + [lead]
        row = jnp.concatenate(
            [jnp.concatenate(blocks[i : i + 2], axis=1) for i in range(0, slots + 1, 2)], axis=1
        )
        high, low = split(row)
        half = high.shape[0]
        out[q, :half] = high
        out[q, half:] = low


def pack(couplings, lead_sites, lead_sigma, info):
    layers, cross_local, slots, size, _ = couplings.shape
    contacts = lead_sigma.shape[0]
    body = functools.partial(pack_kernel, contacts // 2, cross_local, layers, slots)
    return pl.pallas_call(
        body,
        grid_spec=pltpu.PrefetchScalarGridSpec(
            num_scalar_prefetch=2,
            grid=(layers,),
            in_specs=[
                pl.BlockSpec((1, cross_local, slots, size, size), lambda i, *_: (i, 0, 0, 0, 0)),
                pl.BlockSpec((contacts, size, size), lambda i, *_: (0, 0, 0)),
            ],
            out_specs=pl.BlockSpec(
                (cross_local, 2 * size, (slots + 1) * size), lambda i, *_: (i, 0, 0)
            ),
        ),
        out_shape=jax.ShapeDtypeStruct(
            (layers * cross_local, 2 * size, (slots + 1) * size), jnp.bfloat16
        ),
        compiler_params=pltpu.CompilerParams(vmem_limit_bytes=VMEM_LIMIT),
        name="pack",
    )(info, lead_sites, couplings, lead_sigma)


def step_kernel(
    first, slots, info, index, packed, own, other, edge_own, edge_other, before, out, field
):
    layers, cross_local, size, columns = own.shape
    total = 2 * cross_local
    mine = info[0] * cross_local
    theirs = (1 - info[0]) * cross_local

    def put(place, x):
        high, low = split(x)
        field[place, :, :columns] = high
        field[place, :, columns:] = low

    for layer in range(layers):
        for q in range(cross_local):
            put((layer + 1) * total + mine + q, own[layer, q])
            put((layer + 1) * total + theirs + q, other[layer, q])
    for q in range(cross_local):
        put(mine + q, edge_own[0, q])
        put(theirs + q, edge_other[0, q])
        put((layers + 1) * total + mine + q, edge_own[1, q])
        put((layers + 1) * total + theirs + q, edge_other[1, q])
    for layer in range(layers):
        for q in range(cross_local):
            row = layer * cross_local + q
            picked = jnp.concatenate(
                [field[index[row * slots + j]] for j in range(slots)], axis=0
            )
            acc = jnp.dot(packed[row], picked, preferred_element_type=jnp.float32)
            acc = acc[:, :columns] + acc[:, columns:]
            applied = acc[:size] + acc[size:]
            value = (applied - center_shift * own[layer, q]) * (1.0 / half_range)
            if not first:
                value = 2.0 * value - before[layer, q]
            out[layer, q] = value


def step(packed, index, info, own, other, edge_own, edge_other, before, first):
    layers, cross_local, size, columns = own.shape
    rows, _, depth = packed.shape
    slots = depth // size
    whole = pl.BlockSpec(memory_space=pltpu.VMEM)
    scalar = pl.BlockSpec(memory_space=pltpu.SMEM)
    return pl.pallas_call(
        functools.partial(step_kernel, first, slots),
        in_specs=[scalar, scalar] + [whole] * 6,
        out_specs=whole,
        out_shape=jax.ShapeDtypeStruct(own.shape, jnp.float32),
        scratch_shapes=[
            pltpu.VMEM(((layers + 2) * 2 * cross_local, size, 2 * columns), jnp.bfloat16)
        ],
        cost_estimate=pl.CostEstimate(
            flops=8 * rows * size * depth * columns, bytes_accessed=6 << 20, transcendentals=0
        ),
        compiler_params=pltpu.CompilerParams(vmem_limit_bytes=VMEM_LIMIT),
        name="step",
    )(info, index, packed, own, other, edge_own, edge_other, before)


def factor(block):
    size = block.shape[0]
    tall = 8
    tiles = size // tall
    lanes = lax.broadcasted_iota(jnp.int32, (tall, size), 1)
    sub = lax.broadcasted_iota(jnp.int32, (tall, size), 0)
    gram = [block[tall * t : tall * (t + 1)] for t in range(tiles)]
    unit = [jnp.where(lanes == sub + tall * t, 1.0, 0.0) for t in range(tiles)]

    def spread(row):
        return jnp.broadcast_to(row, (tall, size))

    for p in range(tiles):
        cols = [
            [
                jnp.broadcast_to(gram[t][:, tall * p + c : tall * p + c + 1], (tall, size))
                for t in range(p, tiles)
            ]
            for c in range(tall)
        ]
        scales = []
        for c in range(tall):
            scale = lax.rsqrt(spread(cols[c][0][c : c + 1]))
            scales.append(scale)
            cols[c] = [x * scale for x in cols[c]]
            cols[c][0] = jnp.where(sub > c, cols[c][0], 0.0)
            for d in range(c + 1, tall):
                weight = spread(cols[c][0][d : d + 1])
                cols[d] = [x - m * weight for x, m in zip(cols[d], cols[c])]
        for c in range(tall):
            row_gram = spread(gram[p][c : c + 1]) * scales[c]
            row_unit = spread(unit[p][c : c + 1]) * scales[c]
            gram[p] = jnp.where(sub == c, row_gram, gram[p] - cols[c][0] * row_gram)
            unit[p] = jnp.where(sub == c, row_unit, unit[p] - cols[c][0] * row_unit)
            for t in range(p + 1, tiles):
                m = cols[c][t - p]
                gram[t] = gram[t] - m * row_gram
                unit[t] = unit[t] - m * row_unit
    upper = [jnp.where(lanes >= sub + tall * t, gram[t], 0.0) for t in range(tiles)]
    return jnp.concatenate(upper, axis=0), jnp.concatenate(unit, axis=0)


def dot(a, b, dims=((1,), (0,))):
    return lax.dot_general(
        a, b, (dims, ((), ())), precision=HIGHEST, preferred_element_type=jnp.float32
    )


def column_kernel(place, *refs):
    if place:
        gram, inverse, upper_out, inverse_out = refs
    else:
        gram, upper_out, inverse_out = refs
    size = gram.shape[1]
    split_at = place * size
    corner = gram[split_at:, :]
    if place:
        known = inverse[...]
        above = dot(known, gram[:split_at, :], ((0,), (0,)))
        corner = corner - dot(above, above, ((0,), (0,)))
        carried = dot(known, above)
    upper, lower_inverse = factor(corner)
    upper_inverse = lower_inverse.T
    if place:
        upper_out[:split_at, :] = above
        inverse_out[:split_at, :] = -dot(carried, upper_inverse)
    upper_out[split_at:, :] = upper
    inverse_out[split_at:, :] = upper_inverse


def column(place, gram, inverse):
    whole = pl.BlockSpec(memory_space=pltpu.VMEM)
    args = (gram, inverse) if place else (gram,)
    shape = jax.ShapeDtypeStruct(gram.shape, jnp.float32)
    return pl.pallas_call(
        functools.partial(column_kernel, place),
        in_specs=[whole] * len(args),
        out_specs=[whole, whole],
        out_shape=[shape, shape],
        compiler_params=pltpu.CompilerParams(vmem_limit_bytes=VMEM_LIMIT),
        cost_estimate=pl.CostEstimate(flops=1 << 23, bytes_accessed=1 << 19, transcendentals=128),
        name="column",
    )(*args)


def total(x, axes):
    count = math.prod(lax.axis_size(a) for a in axes)
    shares = x.reshape(count, -1) if x.size // count % 1024 else x.reshape(count, -1, x.shape[-1])
    parts = lax.all_to_all(shares, axes, 0, 0, tiled=True)
    mine = jnp.sum(parts, axis=0, keepdims=True)
    copies = jnp.broadcast_to(mine, shares.shape)
    return lax.all_to_all(copies, axes, 0, 0, tiled=True).reshape(x.shape)


def local(sources, couplings, block_cols, lead_sites, lead_sigma):
    layers, cross_local, size, columns = sources.shape
    cross_count = lax.axis_size("cross")
    trans_count = lax.axis_size("trans")
    cross_total = cross_local * cross_count
    trans_place = lax.axis_index("trans")
    cross_place = lax.axis_index("cross")
    info = jnp.stack(
        [
            cross_place,
            (trans_place == 0).astype(jnp.int32),
            (trans_place == trans_count - 1).astype(jnp.int32),
        ]
    ).astype(jnp.int32)
    layer_base = jnp.arange(layers, dtype=jnp.int32)[:, None, None] * cross_total
    self_cols = (cross_total + cross_place * cross_local + jnp.arange(cross_local, dtype=jnp.int32))
    self_cols = jnp.broadcast_to(self_cols[None, :, None], (layers, cross_local, 1))
    index = (layer_base + jnp.concatenate([block_cols, self_cols], axis=2)).reshape(-1)
    packed = pack(couplings, lead_sites, lead_sigma, info)

    forward = [(i, i + 1) for i in range(trans_count - 1)]
    backward = [(i + 1, i) for i in range(trans_count - 1)]
    swap = [(0, 1), (1, 0)]

    powers = [sources]
    uppers = []
    inverses = []
    inverse = None
    for k in range(S + 1):
        field = powers[k]
        if k < S:
            low = lax.ppermute(field[layers - 1 :], "trans", forward)
            high = lax.ppermute(field[:1], "trans", backward)
            other = lax.ppermute(field, "cross", swap)
            edge_own = jnp.concatenate([low, high], axis=0)
            edge_other = lax.ppermute(edge_own, "cross", swap)
        krylov = jnp.concatenate([x.reshape(-1, columns) for x in powers], axis=1)
        part = lax.dot_general(
            krylov, field.reshape(-1, columns), (((0,), (0,)), ((), ())), precision=HIGH
        )
        gram = total(part, ("trans", "cross"))
        upper_col, inverse_col = column(k, gram, inverse)
        fill = ((0, (S - k) * columns), (0, 0))
        uppers.append(jnp.pad(upper_col, fill))
        inverses.append(jnp.pad(inverse_col, fill))
        if k < S:
            inverse = jnp.concatenate([x[: (k + 1) * columns] for x in inverses], axis=1)
            before = powers[k - 1] if k else field
            powers.append(
                step(packed, index, info, field, other, edge_own, edge_other, before, k == 0)
            )
    scale_rows = math.sqrt(trans_count * layers * cross_total * size)
    solver = jnp.concatenate(inverses, axis=1) * scale_rows
    basis = lax.dot_general(krylov, solver, (((1,), (0,)), ((), ())), precision=HIGH)
    basis = basis.astype(jnp.bfloat16).reshape(layers, cross_local, size, (S + 1) * columns)
    return basis, jnp.concatenate(uppers, axis=1) / scale_rows


def solution(mesh):
    return jax.shard_map(
        local,
        mesh=mesh,
        in_specs=(
            P(("energy", "trans"), "cross", None, None),
            P(("energy", "trans"), "cross", None, None, None),
            P("trans", "cross", None),
            P(),
            P("energy", None, None),
        ),
        out_specs=(P(("energy", "trans"), "cross", None, None), P("energy", None)),
        check_vma=False,
    )
```

```python
import functools
import math

import jax
import jax.numpy as jnp
from jax import lax
from jax.experimental import pallas as pl
from jax.experimental.pallas import tpu as pltpu
from jax.sharding import PartitionSpec as P

S = 3
center_shift = 2.0
half_range = 1.6
HIGHEST = lax.Precision.HIGHEST
VMEM_LIMIT = 48 * 1024 * 1024


def split(x):
    high = x.astype(jnp.bfloat16)
    low = (x - high.astype(jnp.float32)).astype(jnp.bfloat16)
    return high, low


def pack_kernel(count, cross_local, layers, slots, info, sites, couplings, sigma, out):
    layer = pl.program_id(0)
    first = jnp.logical_and(layer == 0, info[1] == 1)
    last = jnp.logical_and(layer == layers - 1, info[2] == 1)
    for q in range(cross_local):
        place = info[0] * cross_local + q
        lead = None
        for k in range(2 * count):
            flag = first if k < count else last
            weight = jnp.where(jnp.logical_and(flag, sites[k] == place), -1.0, 0.0)
            term = sigma[k] * weight
            lead = term if lead is None else lead + term
        blocks = [couplings[0, q, j] for j in range(slots)] + [lead]
        row = jnp.concatenate(
            [jnp.concatenate(blocks[i : i + 2], axis=1) for i in range(0, slots + 1, 2)], axis=1
        )
        high, low = split(row)
        half = high.shape[0]
        out[q, :half] = high
        out[q, half:] = low


def pack(couplings, lead_sites, lead_sigma, info):
    layers, cross_local, slots, size, _ = couplings.shape
    contacts = lead_sigma.shape[0]
    body = functools.partial(pack_kernel, contacts // 2, cross_local, layers, slots)
    return pl.pallas_call(
        body,
        grid_spec=pltpu.PrefetchScalarGridSpec(
            num_scalar_prefetch=2,
            grid=(layers,),
            in_specs=[
                pl.BlockSpec((1, cross_local, slots, size, size), lambda i, *_: (i, 0, 0, 0, 0)),
                pl.BlockSpec((contacts, size, size), lambda i, *_: (0, 0, 0)),
            ],
            out_specs=pl.BlockSpec(
                (cross_local, 2 * size, (slots + 1) * size), lambda i, *_: (i, 0, 0)
            ),
        ),
        out_shape=jax.ShapeDtypeStruct(
            (layers * cross_local, 2 * size, (slots + 1) * size), jnp.bfloat16
        ),
        compiler_params=pltpu.CompilerParams(vmem_limit_bytes=VMEM_LIMIT),
        name="pack",
    )(info, lead_sites, couplings, lead_sigma)


def step_kernel(first, last, slots, info, cols, packed, own, other, *refs):
    edges, refs = refs[:4], refs[4:]
    before, refs = (None, refs) if first else (refs[0], refs[1:])
    out, field = refs[0], refs[-1]
    layers, cross_local, size, columns = own.shape
    total = 2 * cross_local
    mine = info[0] * cross_local
    theirs = (1 - info[0]) * cross_local

    def put(place, x):
        high, low = split(x)
        field[place, :, :columns] = high
        field[place, :, columns:] = low

    for layer in range(layers):
        for q in range(cross_local):
            put((layer + 1) * total + mine + q, own[layer, q])
            put((layer + 1) * total + theirs + q, other[layer, q])
    low_own, low_other, high_own, high_other = edges
    for q in range(cross_local):
        put(mine + q, low_own[0, q])
        put(theirs + q, low_other[0, q])
        put((layers + 1) * total + mine + q, high_own[0, q])
        put((layers + 1) * total + theirs + q, high_other[0, q])
    for layer in range(layers):
        for q in range(cross_local):
            row = layer * cross_local + q
            places = [cols[layer, q, j] for j in range(slots)] + [total + mine + q]
            picked = jnp.concatenate([field[layer * total + c] for c in places], axis=0)
            acc = jnp.dot(packed[row], picked, preferred_element_type=jnp.float32)
            acc = acc[:, :columns] + acc[:, columns:]
            applied = acc[:size] + acc[size:]
            value = (applied - center_shift * own[layer, q]) * (1.0 / half_range)
            if not first:
                value = 2.0 * value - before[layer, q]
            out[layer, q] = value
            if not last and layer == 0:
                refs[1][0, q] = value
            if not last and layer == layers - 1:
                refs[2][0, q] = value


def step(packed, cols, info, own, other, edges, before, last):
    layers, cross_local, size, columns = own.shape
    rows, _, depth = packed.shape
    whole = pl.BlockSpec(memory_space=pltpu.VMEM)
    scalar = pl.BlockSpec(memory_space=pltpu.SMEM)
    args = [packed, own, other, *edges] + ([] if before is None else [before])
    edge = jax.ShapeDtypeStruct((1,) + own.shape[1:], jnp.float32)
    shapes = [jax.ShapeDtypeStruct(own.shape, jnp.float32)] + ([] if last else [edge, edge])
    return pl.pallas_call(
        functools.partial(step_kernel, before is None, last, cols.shape[2]),
        in_specs=[scalar, scalar] + [whole] * len(args),
        out_specs=[whole] * len(shapes),
        out_shape=shapes,
        scratch_shapes=[
            pltpu.VMEM(((layers + 2) * 2 * cross_local, size, 2 * columns), jnp.bfloat16)
        ],
        cost_estimate=pl.CostEstimate(
            flops=8 * rows * size * depth * columns, bytes_accessed=6 << 20, transcendentals=0
        ),
        compiler_params=pltpu.CompilerParams(vmem_limit_bytes=VMEM_LIMIT),
        name="step",
    )(info, cols, *args)


def gram_kernel(pairs, count, *refs):
    if len(refs) > count + 3:
        info, refs = refs[0], refs[1:]
        outs = refs[count : count + 2]
    else:
        info, outs = None, refs[count : count + 1]
    powers, held = refs[:count], refs[-1]
    columns = outs[0].shape[-1] // len(pairs)

    for j in range(count):
        high, low = split(powers[j][...].reshape(-1, columns))
        held[j, :, :columns] = high
        held[j, :, columns:] = low
    if info is not None:
        half = columns // 2
        mine = pl.multiple_of(info[0] * half, half)
        theirs = pl.multiple_of((1 - info[0]) * half, half)
        block = refs[-2]
    for place, (i, j) in enumerate(pairs):
        acc = lax.dot_general(
            held[i], held[j], (((0,), (0,)), ((), ())), preferred_element_type=jnp.float32
        )
        acc = acc[:, :columns] + acc[:, columns:]
        acc = acc[:columns] + acc[columns:]
        at = slice(place * columns, (place + 1) * columns)
        if info is None:
            outs[0][:, at] = acc
        else:
            block[...] = acc
            outs[0][:, at] = block[pl.ds(mine, half), :]
            outs[1][:, at] = block[pl.ds(theirs, half), :]


def gram_blocks(powers, pairs, info=None):
    columns = powers[0].shape[-1]
    rows = powers[0].size // columns
    whole = pl.BlockSpec(memory_space=pltpu.VMEM)
    cut = 1 if info is None else 2
    shape = jax.ShapeDtypeStruct((columns // cut, len(pairs) * columns), jnp.float32)
    scalars = [] if info is None else [info]
    return pl.pallas_call(
        functools.partial(gram_kernel, pairs, len(powers)),
        in_specs=[pl.BlockSpec(memory_space=pltpu.SMEM)] * len(scalars) + [whole] * len(powers),
        out_specs=[whole] * cut,
        out_shape=[shape] * cut,
        scratch_shapes=[pltpu.VMEM((columns, columns), jnp.float32)] * (cut - 1)
        + [pltpu.VMEM((len(powers), rows, 2 * columns), jnp.bfloat16)],
        cost_estimate=pl.CostEstimate(
            flops=8 * rows * columns * columns * len(pairs),
            bytes_accessed=len(powers) * rows * columns * 4,
            transcendentals=0,
        ),
        compiler_params=pltpu.CompilerParams(vmem_limit_bytes=VMEM_LIMIT),
        name="gram",
    )(*scalars, *powers)


def factor(block):
    size = block.shape[0]
    tall = 8
    tiles = size // tall
    lanes = lax.broadcasted_iota(jnp.int32, (tall, size), 1)
    sub = lax.broadcasted_iota(jnp.int32, (tall, size), 0)
    gram = [block[tall * t : tall * (t + 1)] for t in range(tiles)]
    unit = [jnp.where(lanes == sub + tall * t, 1.0, 0.0) for t in range(tiles)]

    def spread(row):
        return jnp.broadcast_to(row, (tall, size))

    for p in range(tiles):
        cols = [
            [
                jnp.broadcast_to(gram[t][:, tall * p + c : tall * p + c + 1], (tall, size))
                for t in range(p, tiles)
            ]
            for c in range(tall)
        ]
        scales = []
        for c in range(tall):
            scale = lax.rsqrt(spread(cols[c][0][c : c + 1]))
            scales.append(scale)
            cols[c] = [x * scale for x in cols[c]]
            cols[c][0] = jnp.where(sub > c, cols[c][0], 0.0)
            for d in range(c + 1, tall):
                weight = spread(cols[c][0][d : d + 1])
                cols[d] = [x - m * weight for x, m in zip(cols[d], cols[c])]
        for c in range(tall):
            row_gram = spread(gram[p][c : c + 1]) * scales[c]
            row_unit = spread(unit[p][c : c + 1]) * scales[c]
            gram[p] = jnp.where(sub == c, row_gram, gram[p] - cols[c][0] * row_gram)
            unit[p] = jnp.where(sub == c, row_unit, unit[p] - cols[c][0] * row_unit)
            for t in range(p + 1, tiles):
                m = cols[c][t - p]
                gram[t] = gram[t] - m * row_gram
                unit[t] = unit[t] - m * row_unit
    upper = [jnp.where(lanes >= sub + tall * t, gram[t], 0.0) for t in range(tiles)]
    return jnp.concatenate(upper, axis=0), jnp.concatenate(unit, axis=0)


def dot(a, b, dims=((1,), (0,))):
    return lax.dot_general(
        a, b, (dims, ((), ())), precision=HIGHEST, preferred_element_type=jnp.float32
    )


def column_kernel(place, scale, offset, *refs):
    if scale is None:
        gram, refs = refs[0], refs[1:]
        size = gram.shape[0]
    else:
        info, own, other, refs, gram = *refs[:3], refs[3:-1], refs[-1]
        half = own.shape[0]
        size = 2 * half
        gram[pl.ds(pl.multiple_of(info[0] * half, half), half), :] = own[...]
        gram[pl.ds(pl.multiple_of((1 - info[0]) * half, half), half), :] = other[...]
    inverses, refs = refs[:place], refs[place:]

    def part(m):
        return slice(m * size, (m + 1) * size)

    corner = gram[:, part(offset + place)]
    above = [
        dot(inverses[i][...], gram[:, offset * size : (offset + i + 1) * size], ((0,), (1,)))
        for i in range(place)
    ]
    for x in above:
        corner = corner - dot(x, x, ((0,), (0,)))
    carried = []
    for m in range(place):
        terms = [dot(inverses[i][part(m), :], above[i]) for i in range(m, place)]
        carried.append(functools.reduce(lambda x, y: x + y, terms))
    upper, lower_inverse = factor(corner)
    upper_inverse = lower_inverse.T
    if scale is None:
        upper_out, inverse_out = refs
    else:
        uppers, (result, inverse_out) = refs[:place], refs[place:]
        result[...] = jnp.zeros_like(result)
        for i in range(place):
            result[: (i + 1) * size, part(i)] = uppers[i][...] * scale
        upper_out = result.at[:, part(place)]
        above = [x * scale for x in above]
        upper = upper * scale
    for m in range(place):
        upper_out[part(m), :] = above[m]
        inverse_out[part(m), :] = -dot(carried[m], upper_inverse)
    upper_out[part(place), :] = upper
    inverse_out[part(place), :] = upper_inverse


def column(gram, inverses, offset=0, info=None, uppers=(), scale=None):
    whole = pl.BlockSpec(memory_space=pltpu.VMEM)
    place = len(inverses)
    args = [gram] if scale is None else list(gram)
    size = args[0].shape[0] * len(args)
    specs = [whole] * (len(args) + place + len(uppers))
    args += [*inverses, *uppers]
    shape = jax.ShapeDtypeStruct(((place + 1) * size, size), jnp.float32)
    square = jax.ShapeDtypeStruct(((place + 1) * size,) * 2, jnp.float32)
    scratch = []
    if scale is not None:
        args = [info] + args
        specs = [pl.BlockSpec(memory_space=pltpu.SMEM)] + specs
        scratch = [pltpu.VMEM((size, (place + 1) * size), jnp.float32)]
    return pl.pallas_call(
        functools.partial(column_kernel, place, scale, offset),
        in_specs=specs,
        out_specs=[whole, whole],
        out_shape=[shape if scale is None else square, shape],
        scratch_shapes=scratch,
        compiler_params=pltpu.CompilerParams(vmem_limit_bytes=VMEM_LIMIT),
        cost_estimate=pl.CostEstimate(flops=1 << 23, bytes_accessed=1 << 19, transcendentals=128),
        name="column",
    )(*args)


def basis_kernel(scale, count, *refs):
    powers, inverses, (out, high, low) = refs[:count], refs[count : 2 * count], refs[2 * count :]
    columns = powers[0].shape[-1]

    @pl.when(pl.program_id(0) == 0)
    def _():
        high[...] = jnp.zeros_like(high)
        low[...] = jnp.zeros_like(low)
        for j, inverse in enumerate(inverses):
            a, b = split(inverse[...] * scale)
            high[: (j + 1) * columns, j * columns : (j + 1) * columns] = a
            low[: (j + 1) * columns, j * columns : (j + 1) * columns] = b

    pairs = [split(p[...].reshape(-1, columns)) for p in powers]
    wide = 2 * columns
    for start in range(0, count * columns, wide):
        stop = min(start + wide, count * columns)
        left_high = jnp.concatenate([p[0] for p in pairs[: stop // columns]], axis=1)
        left_low = jnp.concatenate([p[1] for p in pairs[: stop // columns]], axis=1)
        right = high[:stop, start:stop]
        acc = jnp.dot(left_high, right, preferred_element_type=jnp.float32)
        acc = acc + jnp.dot(left_low, right, preferred_element_type=jnp.float32)
        acc = acc + jnp.dot(left_high, low[:stop, start:stop], preferred_element_type=jnp.float32)
        out[:, :, :, start:stop] = acc.astype(jnp.bfloat16).reshape(out.shape[:3] + (stop - start,))


def basis_of(powers, inverses, scale):
    layers, cross_local, size, columns = powers[0].shape
    count = len(powers)
    full = count * columns
    return pl.pallas_call(
        functools.partial(basis_kernel, scale, count),
        grid=(layers,),
        in_specs=[pl.BlockSpec((1, cross_local, size, columns), lambda i: (i, 0, 0, 0))] * count
        + [pl.BlockSpec(x.shape, lambda i: (0, 0)) for x in inverses],
        out_specs=pl.BlockSpec((1, cross_local, size, full), lambda i: (i, 0, 0, 0)),
        out_shape=jax.ShapeDtypeStruct((layers, cross_local, size, full), jnp.bfloat16),
        scratch_shapes=[pltpu.VMEM((full, full), jnp.bfloat16)] * 2,
        compiler_params=pltpu.CompilerParams(vmem_limit_bytes=VMEM_LIMIT),
        name="basis",
    )(*powers, *inverses)


def total(x, axis):
    count = lax.axis_size(axis)
    shares = x.reshape(count, -1) if x.shape[0] % count else x.reshape(count, -1, x.shape[1])
    parts = lax.all_to_all(shares, axis, 0, 0, tiled=True)
    mine = jnp.sum(parts, axis=0, keepdims=True)
    copies = jnp.broadcast_to(mine, shares.shape)
    return lax.all_to_all(copies, axis, 0, 0, tiled=True).reshape(x.shape)


def local(sources, couplings, block_cols, lead_sites, lead_sigma):
    layers, cross_local, size, columns = sources.shape
    cross_count = lax.axis_size("cross")
    trans_count = lax.axis_size("trans")
    trans_place = lax.axis_index("trans")
    info = jnp.stack(
        [
            lax.axis_index("cross"),
            (trans_place == 0).astype(jnp.int32),
            (trans_place == trans_count - 1).astype(jnp.int32),
        ]
    ).astype(jnp.int32)
    packed = pack(couplings, lead_sites, lead_sigma, info)

    forward = [(i, i + 1) for i in range(trans_count - 1)]
    backward = [(i + 1, i) for i in range(trans_count - 1)]
    swap = [(0, 1), (1, 0)]
    scale_rows = math.sqrt(trans_count * layers * cross_local * cross_count * size)

    powers = [sources]
    first_layer, last_layer = sources[:1], sources[layers - 1 :]
    sums = []
    for k in range(S):
        field = powers[k]
        low = lax.ppermute(last_layer, "trans", forward)
        high = lax.ppermute(first_layer, "trans", backward)
        other = lax.ppermute(field, "cross", swap)
        edges = (low, lax.ppermute(low, "cross", swap), high, lax.ppermute(high, "cross", swap))
        if k == 1:
            part = gram_blocks(powers, ((0, 0), (1, 0), (1, 1)))[0]
            sums.append(lax.psum(part, ("trans", "cross")))
        if k == 2:
            part = gram_blocks(powers, ((2, 0), (2, 1), (2, 2)))[0]
            sums.append(lax.psum(part, ("cross", "trans")))
        before = powers[k - 1] if k else None
        got = step(packed, block_cols, info, field, other, edges, before, k == S - 1)
        powers.append(got[0])
        if k < S - 1:
            first_layer, last_layer = got[1:]
    mine, theirs = gram_blocks(powers, tuple((S, j) for j in range(S + 1)), info)
    mine = total(mine + lax.ppermute(theirs, "cross", swap), "trans")
    theirs = lax.ppermute(mine, "cross", swap)

    upper_0, inverse_0 = column(sums[0][:, :columns], [])
    upper_1, inverse_1 = column(sums[0], [inverse_0], 1)
    upper_2, inverse_2 = column(sums[1], [inverse_0, inverse_1])
    inverses = [inverse_0, inverse_1, inverse_2]
    uppers = [upper_0, upper_1, upper_2]
    r_factor, inverse_3 = column((mine, theirs), inverses, 0, info, uppers, 1.0 / scale_rows)
    return basis_of(powers, inverses + [inverse_3], scale_rows), r_factor


def solution(mesh):
    return jax.shard_map(
        local,
        mesh=mesh,
        in_specs=(
            P(("energy", "trans"), "cross", None, None),
            P(("energy", "trans"), "cross", None, None, None),
            P("trans", "cross", None),
            P(),
            P("energy", None, None),
        ),
        out_specs=(P(("energy", "trans"), "cross", None, None), P("energy", None)),
        check_vma=False,
    )
```

```python
import functools
import math

import jax
import jax.numpy as jnp
from jax import lax
from jax.experimental import pallas as pl
from jax.experimental.pallas import tpu as pltpu
from jax.sharding import PartitionSpec as P

S = 3
center_shift = 2.0
half_range = 1.6
HIGHEST = lax.Precision.HIGHEST
VMEM_LIMIT = 48 * 1024 * 1024


def estimate(us):
    return pl.CostEstimate(flops=int(us * 1.15e9), bytes_accessed=0, transcendentals=0)


def split(x):
    high = x.astype(jnp.bfloat16)
    low = (x - high.astype(jnp.float32)).astype(jnp.bfloat16)
    return high, low


def pack_kernel(count, cross_local, layers, slots, info, sites, couplings, sigma, out):
    layer = pl.program_id(0)
    first = jnp.logical_and(layer == 0, info[1] == 1)
    last = jnp.logical_and(layer == layers - 1, info[2] == 1)
    for q in range(cross_local):
        place = info[0] * cross_local + q
        lead = None
        for k in range(2 * count):
            flag = first if k < count else last
            weight = jnp.where(jnp.logical_and(flag, sites[k] == place), -1.0, 0.0)
            term = sigma[k] * weight
            lead = term if lead is None else lead + term
        blocks = [couplings[0, q, j] for j in range(slots)] + [lead]
        row = jnp.concatenate(
            [jnp.concatenate(blocks[i : i + 2], axis=1) for i in range(0, slots + 1, 2)], axis=1
        )
        high, low = split(row)
        half = high.shape[0]
        out[q, :half] = high
        out[q, half:] = low


def pack(couplings, lead_sites, lead_sigma, info):
    layers, cross_local, slots, size, _ = couplings.shape
    contacts = lead_sigma.shape[0]
    body = functools.partial(pack_kernel, contacts // 2, cross_local, layers, slots)
    return pl.pallas_call(
        body,
        grid_spec=pltpu.PrefetchScalarGridSpec(
            num_scalar_prefetch=2,
            grid=(layers,),
            in_specs=[
                pl.BlockSpec((1, cross_local, slots, size, size), lambda i, *_: (i, 0, 0, 0, 0)),
                pl.BlockSpec((contacts, size, size), lambda i, *_: (0, 0, 0)),
            ],
            out_specs=pl.BlockSpec(
                (cross_local, 2 * size, (slots + 1) * size), lambda i, *_: (i, 0, 0)
            ),
        ),
        out_shape=jax.ShapeDtypeStruct(
            (layers * cross_local, 2 * size, (slots + 1) * size), jnp.bfloat16
        ),
        compiler_params=pltpu.CompilerParams(vmem_limit_bytes=VMEM_LIMIT),
        cost_estimate=estimate(1.5),
        name="pack",
    )(info, lead_sites, couplings, lead_sigma)


def step_kernel(first, last, slots, info, cols, packed, own, other, *refs):
    edges, refs = refs[:4], refs[4:]
    before, refs = (None, refs) if first else (refs[0], refs[1:])
    out, field = refs[0], refs[-1]
    layers, cross_local, size, columns = own.shape
    total = 2 * cross_local
    mine = info[0] * cross_local
    theirs = (1 - info[0]) * cross_local

    def put(place, x):
        high, low = split(x)
        field[place, :, :columns] = high
        field[place, :, columns:] = low

    for layer in range(layers):
        for q in range(cross_local):
            put((layer + 1) * total + mine + q, own[layer, q])
            put((layer + 1) * total + theirs + q, other[layer, q])
    even = info[3]
    for pair, place in enumerate((even, 1 - even)):
        for q in range(cross_local):
            put(place * (layers + 1) * total + mine + q, edges[2 * pair][0, q])
            put(place * (layers + 1) * total + theirs + q, edges[2 * pair + 1][0, q])
    for layer in range(layers):
        for q in range(cross_local):
            row = layer * cross_local + q
            places = [cols[layer, q, j] for j in range(slots)] + [total + mine + q]
            picked = jnp.concatenate([field[layer * total + c] for c in places], axis=0)
            acc = jnp.dot(packed[row], picked, preferred_element_type=jnp.float32)
            acc = acc[:, :columns] + acc[:, columns:]
            applied = acc[:size] + acc[size:]
            value = (applied - center_shift * own[layer, q]) * (1.0 / half_range)
            if not first:
                value = 2.0 * value - before[layer, q]
            out[layer, q] = value
    if not last:
        refs[1][0] = out[even * (layers - 1)]
        refs[2][0] = out[(1 - even) * (layers - 1)]


def step(packed, cols, info, own, other, edges, before, last):
    layers, cross_local, size, columns = own.shape
    rows, _, depth = packed.shape
    whole = pl.BlockSpec(memory_space=pltpu.VMEM)
    scalar = pl.BlockSpec(memory_space=pltpu.SMEM)
    args = [packed, own, other, *edges] + ([] if before is None else [before])
    edge = jax.ShapeDtypeStruct((1,) + own.shape[1:], jnp.float32)
    shapes = [jax.ShapeDtypeStruct(own.shape, jnp.float32)] + ([] if last else [edge, edge])
    return pl.pallas_call(
        functools.partial(step_kernel, before is None, last, cols.shape[2]),
        in_specs=[scalar, scalar] + [whole] * len(args),
        out_specs=[whole] * len(shapes),
        out_shape=shapes,
        scratch_shapes=[
            pltpu.VMEM(((layers + 2) * 2 * cross_local, size, 2 * columns), jnp.bfloat16)
        ],
        cost_estimate=estimate(1.7),
        compiler_params=pltpu.CompilerParams(vmem_limit_bytes=VMEM_LIMIT),
        name="step",
    )(info, cols, *args)


def gram_kernel(pairs, info, *refs):
    *powers, mine, theirs, block, held = refs
    columns = mine.shape[1]
    half = columns // 2
    for j, power in enumerate(powers):
        high, low = split(power[...].reshape(-1, columns))
        held[j, :, :columns] = high
        held[j, :, columns:] = low
    for place, (i, j) in enumerate(pairs):
        acc = lax.dot_general(
            held[i], held[j], (((0,), (0,)), ((), ())), preferred_element_type=jnp.float32
        )
        acc = acc[:, :columns] + acc[:, columns:]
        block[place] = acc[:columns] + acc[columns:]
        for core, out in ((info[0], mine), (1 - info[0], theirs)):
            rows = pl.ds(pl.multiple_of(core * half, half), half)
            out[place * half : (place + 1) * half, :] = block[place, rows, :]
    used = len(pairs) * half
    if used < mine.shape[0]:
        for out in (mine, theirs):
            out[used:, :] = jnp.zeros((mine.shape[0] - used, columns), jnp.float32)


def gram_blocks(powers, pairs, info, count):
    columns = powers[0].shape[-1]
    rows = powers[0].size // columns
    whole = pl.BlockSpec(memory_space=pltpu.VMEM)
    tall = share(len(pairs), columns, count) * count
    return pl.pallas_call(
        functools.partial(gram_kernel, pairs),
        in_specs=[pl.BlockSpec(memory_space=pltpu.SMEM)] + [whole] * len(powers),
        out_specs=[whole] * 2,
        out_shape=[jax.ShapeDtypeStruct((tall, columns), jnp.float32)] * 2,
        scratch_shapes=[
            pltpu.VMEM((len(pairs), columns, columns), jnp.float32),
            pltpu.VMEM((len(powers), rows, 2 * columns), jnp.bfloat16),
        ],
        cost_estimate=estimate(1.4),
        compiler_params=pltpu.CompilerParams(vmem_limit_bytes=VMEM_LIMIT),
        name="gram",
    )(info, *powers)


def share(blocks, columns, count):
    return -(-blocks * (columns // 2) // count)


def message_kernel(done, fresh, *refs):
    *ins, out = refs
    count = out.shape[0]
    if fresh:
        mine, theirs = ins[:2]
    if done:
        parts = ins[-1]
        width = parts.shape[1] - done
        acc = parts[0, width:, :]
        for p in range(1, count):
            acc = acc + parts[p, width:, :]
    for p in range(count):
        if done:
            out[p, :done, :] = acc
        if fresh:
            rows = slice(p * fresh, (p + 1) * fresh)
            out[p, done:, :] = mine[rows, :] + theirs[rows, :]


def message(halves, parts, done, count):
    whole = pl.BlockSpec(memory_space=pltpu.VMEM)
    args = list(halves) + ([] if parts is None else [parts])
    fresh = halves[0].shape[0] // count if halves else 0
    return pl.pallas_call(
        functools.partial(message_kernel, done, fresh),
        in_specs=[whole] * len(args),
        out_specs=whole,
        out_shape=jax.ShapeDtypeStruct((count, done + fresh, args[0].shape[-1]), jnp.float32),
        cost_estimate=estimate(0.3),
        compiler_params=pltpu.CompilerParams(vmem_limit_bytes=VMEM_LIMIT),
        name="message",
    )(*args)


def factor(block):
    size = block.shape[0]
    tall = 8
    tiles = size // tall
    lanes = lax.broadcasted_iota(jnp.int32, (tall, size), 1)
    sub = lax.broadcasted_iota(jnp.int32, (tall, size), 0)
    gram = [block[tall * t : tall * (t + 1)] for t in range(tiles)]
    unit = [jnp.where(lanes == sub + tall * t, 1.0, 0.0) for t in range(tiles)]

    def spread(row):
        return jnp.broadcast_to(row, (tall, size))

    for p in range(tiles):
        cols = [
            [
                jnp.broadcast_to(gram[t][:, tall * p + c : tall * p + c + 1], (tall, size))
                for t in range(p, tiles)
            ]
            for c in range(tall)
        ]
        scales = []
        for c in range(tall):
            scale = lax.rsqrt(spread(cols[c][0][c : c + 1]))
            scales.append(scale)
            cols[c] = [x * scale for x in cols[c]]
            cols[c][0] = jnp.where(sub > c, cols[c][0], 0.0)
            for d in range(c + 1, tall):
                weight = spread(cols[c][0][d : d + 1])
                cols[d] = [x - m * weight for x, m in zip(cols[d], cols[c])]
        for c in range(tall):
            row_gram = spread(gram[p][c : c + 1]) * scales[c]
            row_unit = spread(unit[p][c : c + 1]) * scales[c]
            gram[p] = jnp.where(sub == c, row_gram, gram[p] - cols[c][0] * row_gram)
            unit[p] = jnp.where(sub == c, row_unit, unit[p] - cols[c][0] * row_unit)
            for t in range(p + 1, tiles):
                m = cols[c][t - p]
                gram[t] = gram[t] - m * row_gram
                unit[t] = unit[t] - m * row_unit
    upper = [jnp.where(lanes >= sub + tall * t, gram[t], 0.0) for t in range(tiles)]
    return jnp.concatenate(upper, axis=0), jnp.concatenate(unit, axis=0)


def dot(a, b, dims=((1,), (0,))):
    return lax.dot_general(
        a, b, (dims, ((), ())), precision=HIGHEST, preferred_element_type=jnp.float32
    )


def column_kernel(place, first, row_share, scale, info, own, other, *refs):
    *refs, flat, gram = refs
    known, refs = (None, refs) if place == 0 else (refs[0], refs[1:])
    upper_known, refs = (None, refs) if place == 0 else (refs[0], refs[1:])
    upper_out, inverse_out = refs
    size = gram.shape[0]
    half = size // 2
    count = own.shape[0]
    at = place * size
    for core, source in ((info[0], own), (1 - info[0], other)):
        rows = pl.ds(pl.multiple_of(core * half, half), half)
        for p in range(count):
            flat[p * row_share : (p + 1) * row_share, :] = source[p, :row_share, :]
        for j in range(place + 1):
            gram[rows, j * size : (j + 1) * size] = flat[(first + j) * half : (first + j + 1) * half, :]
    corner = gram[:, at:]
    if place:
        above = dot(known[...], gram[:, :at], ((0,), (1,)))
        corner = corner - dot(above, above, ((0,), (0,)))
        carried = dot(known[...], above)
    upper, lower_inverse = factor(corner)
    upper_inverse = lower_inverse.T
    if place:
        upper_out[:at, :at] = upper_known[...] * scale
        inverse_out[:at, :at] = known[...]
        upper_out[:at, at:] = above * scale
        inverse_out[:at, at:] = -dot(carried, upper_inverse)
        upper_out[at:, :at] = jnp.zeros((size, at), jnp.float32)
        inverse_out[at:, :at] = jnp.zeros((size, at), jnp.float32)
    upper_out[at:, at:] = upper * scale
    inverse_out[at:, at:] = upper_inverse


def column(place, first, blocks, info, own, other, before, scale=1.0):
    whole = pl.BlockSpec(memory_space=pltpu.VMEM)
    count, _, size = own.shape
    row_share = share(blocks, size, count)
    args = [own, other, *before]
    square = jax.ShapeDtypeStruct(((place + 1) * size,) * 2, jnp.float32)
    return pl.pallas_call(
        functools.partial(column_kernel, place, first, row_share, scale),
        in_specs=[pl.BlockSpec(memory_space=pltpu.SMEM)] + [whole] * len(args),
        out_specs=[whole, whole],
        out_shape=[square, square],
        scratch_shapes=[
            pltpu.VMEM((count * row_share, size), jnp.float32),
            pltpu.VMEM((size, (place + 1) * size), jnp.float32),
        ],
        compiler_params=pltpu.CompilerParams(vmem_limit_bytes=VMEM_LIMIT),
        cost_estimate=estimate(4.5),
        name="column",
    )(info, *args)


def basis_kernel(scale, count, *refs):
    *powers, inverse, out, high, low = refs
    columns = powers[0].shape[-1]

    @pl.when(pl.program_id(0) == 0)
    def _():
        high[...], low[...] = split(inverse[...] * scale)

    pairs = [split(p[...].reshape(-1, columns)) for p in powers]
    wide = 2 * columns
    for start in range(0, count * columns, wide):
        stop = min(start + wide, count * columns)
        left_high = jnp.concatenate([p[0] for p in pairs[: stop // columns]], axis=1)
        left_low = jnp.concatenate([p[1] for p in pairs[: stop // columns]], axis=1)
        right = high[:stop, start:stop]
        acc = jnp.dot(left_high, right, preferred_element_type=jnp.float32)
        acc = acc + jnp.dot(left_low, right, preferred_element_type=jnp.float32)
        acc = acc + jnp.dot(left_high, low[:stop, start:stop], preferred_element_type=jnp.float32)
        out[:, :, :, start:stop] = acc.astype(jnp.bfloat16).reshape(out.shape[:3] + (stop - start,))


def basis_of(powers, inverse, scale):
    layers, cross_local, size, columns = powers[0].shape
    count = len(powers)
    full = count * columns
    return pl.pallas_call(
        functools.partial(basis_kernel, scale, count),
        grid=(layers,),
        in_specs=[pl.BlockSpec((1, cross_local, size, columns), lambda i: (i, 0, 0, 0))] * count
        + [pl.BlockSpec(inverse.shape, lambda i: (0, 0))],
        out_specs=pl.BlockSpec((1, cross_local, size, full), lambda i: (i, 0, 0, 0)),
        out_shape=jax.ShapeDtypeStruct((layers, cross_local, size, full), jnp.bfloat16),
        scratch_shapes=[pltpu.VMEM((full, full), jnp.bfloat16)] * 2,
        compiler_params=pltpu.CompilerParams(vmem_limit_bytes=VMEM_LIMIT),
        cost_estimate=estimate(3.0),
        name="basis",
    )(*powers, inverse)


def local(sources, couplings, block_cols, lead_sites, lead_sigma):
    layers, cross_local, size, columns = sources.shape
    cross_count = lax.axis_size("cross")
    count = lax.axis_size("trans")
    place = lax.axis_index("trans")
    even = 1 - place % 2
    info = jnp.stack([lax.axis_index("cross"), place == 0, place == count - 1, even]).astype(jnp.int32)
    packed = pack(couplings, lead_sites, lead_sigma, info)

    near = [(i, i + 1) for i in range(0, count - 1, 2)]
    far = [(i, i + 1) for i in range(1, count - 1, 2)]
    near, far = ([*x, *[(j, i) for i, j in x]] for x in (near, far))
    scale_rows = math.sqrt(count * layers * cross_local * cross_count * size)

    def swap(x):
        return lax.ppermute(x, "cross", [(0, 1), (1, 0)])

    def exchange(x):
        return lax.all_to_all(x, "trans", 0, 0, tiled=True)

    def ahead(pairs, parts, done):
        mine, theirs = gram_blocks(powers, pairs, info, count)
        return exchange(message((mine, swap(theirs)), parts, done, count))

    groups = (((0, 0), (1, 0), (1, 1)), ((2, 0), (2, 1), (2, 2)), tuple((S, j) for j in range(S + 1)))
    shares = [share(len(g), columns, count) for g in groups]
    powers = [sources]
    near_layer = lax.dynamic_slice_in_dim(sources, even * (layers - 1), 1)
    far_layer = lax.dynamic_slice_in_dim(sources, (1 - even) * (layers - 1), 1)
    parts, done = None, 0
    sums = []
    for k in range(S):
        field = powers[k]
        near_edge = lax.ppermute(near_layer, "trans", near)
        far_edge = lax.ppermute(far_layer, "trans", far)
        other = swap(field)
        if k == 0:
            near_edge, far_edge, packed = lax.optimization_barrier((near_edge, far_edge, packed))
        else:
            parts = ahead(groups[k - 1], parts, done)
            done = shares[k - 1]
            sums.append(parts)
        edges = (near_edge, swap(near_edge), far_edge, swap(far_edge))
        before = powers[k - 1] if k else None
        got = step(packed, block_cols, info, field, other, edges, before, k == S - 1)
        powers.append(got[0])
        if k < S - 1:
            near_layer, far_layer = got[1:]
    parts = ahead(groups[2], parts, done)
    first = column(0, 0, 3, info, sums[1], swap(sums[1]), ())
    second = column(1, 1, 3, info, sums[1], swap(sums[1]), first[::-1])
    last = exchange(message((), parts, shares[2], count))
    third = column(2, 0, 3, info, parts, swap(parts), second[::-1])
    r_factor, inverse = column(3, 0, 4, info, last, swap(last), third[::-1], 1.0 / scale_rows)
    return basis_of(powers, inverse, scale_rows), r_factor


def solution(mesh):
    return jax.shard_map(
        local,
        mesh=mesh,
        in_specs=(
            P(("energy", "trans"), "cross", None, None),
            P(("energy", "trans"), "cross", None, None, None),
            P("trans", "cross", None),
            P(),
            P("energy", None, None),
        ),
        out_specs=(P(("energy", "trans"), "cross", None, None), P("energy", None)),
        check_vma=False,
    )
```

```python
import functools
import math

import jax
import jax.numpy as jnp
from jax import lax
from jax.experimental import pallas as pl
from jax.experimental.pallas import tpu as pltpu
from jax.sharding import PartitionSpec as P

S = 3
center_shift = 2.0
half_range = 1.6
VMEM_LIMIT = 16 * 1024 * 1024
PACK_VMEM_LIMIT = 60 * 1024 * 1024


def estimate(us):
    return pl.CostEstimate(flops=int(us * 1.15e9), bytes_accessed=0, transcendentals=0)


def split(x):
    high = x.astype(jnp.bfloat16)
    low = (x - high.astype(jnp.float32)).astype(jnp.bfloat16)
    return high, low


def pack_kernel(count, cross_local, layers, slots, info, couplings, sigma, out):
    layer = pl.program_id(0)
    first = jnp.logical_and(layer == 0, info[1] == 1)
    last = jnp.logical_and(layer == layers - 1, info[2] == 1)
    for q in range(cross_local):
        place = info[0] * cross_local + q
        lead = None
        for k in range(2 * count):
            flag = first if k < count else last
            weight = jnp.where(jnp.logical_and(flag, info[4 + k] == place), -1.0, 0.0)
            term = sigma[k] * weight
            lead = term if lead is None else lead + term
        blocks = [couplings[0, q, j] for j in range(slots)] + [lead]
        row = jnp.concatenate(
            [jnp.concatenate(blocks[i : i + 2], axis=1) for i in range(0, slots + 1, 2)], axis=1
        )
        high, low = split(row)
        half = high.shape[0]
        out[q, :half] = high
        out[q, half:] = low


def pack(couplings, lead_sigma, info):
    layers, cross_local, slots, size, _ = couplings.shape
    contacts = lead_sigma.shape[0]
    body = functools.partial(pack_kernel, contacts // 2, cross_local, layers, slots)
    return pl.pallas_call(
        body,
        grid_spec=pltpu.PrefetchScalarGridSpec(
            num_scalar_prefetch=1,
            grid=(layers,),
            in_specs=[
                pl.BlockSpec((1, cross_local, slots, size, size), lambda i, *_: (i, 0, 0, 0, 0)),
                pl.BlockSpec((contacts, size, size), lambda i, *_: (0, 0, 0)),
            ],
            out_specs=pl.BlockSpec(
                (cross_local, 2 * size, (slots + 1) * size), lambda i, *_: (i, 0, 0)
            ),
        ),
        out_shape=jax.ShapeDtypeStruct(
            (layers * cross_local, 2 * size, (slots + 1) * size), jnp.bfloat16
        ),
        compiler_params=pltpu.CompilerParams(vmem_limit_bytes=PACK_VMEM_LIMIT),
        cost_estimate=estimate(2.5),
        name="pack",
    )(info, couplings, lead_sigma)


def step_kernel(first, last, slots, info, cols, packed, own, other, *refs):
    edges, refs = refs[:4], refs[4:]
    before, refs = (None, refs) if first else (refs[0], refs[1:])
    out, field = refs[0], refs[-1]
    layers, cross_local, size, columns = own.shape
    total = 2 * cross_local
    mine = info[0] * cross_local
    theirs = (1 - info[0]) * cross_local

    def put(place, x):
        high, low = split(x)
        field[place, :, :columns] = high
        field[place, :, columns:] = low

    for layer in range(layers):
        for q in range(cross_local):
            put((layer + 1) * total + mine + q, own[layer, q])
            put((layer + 1) * total + theirs + q, other[layer, q])
    even = info[3]
    for pair, place in enumerate((even, 1 - even)):
        for q in range(cross_local):
            put(place * (layers + 1) * total + mine + q, edges[2 * pair][0, q])
            put(place * (layers + 1) * total + theirs + q, edges[2 * pair + 1][0, q])
    for layer in range(layers):
        for q in range(cross_local):
            row = layer * cross_local + q
            places = [cols[layer, q, j] for j in range(slots)] + [total + mine + q]
            picked = jnp.concatenate([field[layer * total + c] for c in places], axis=0)
            acc = jnp.dot(packed[row], picked, preferred_element_type=jnp.float32)
            acc = acc[:, :columns] + acc[:, columns:]
            applied = acc[:size] + acc[size:]
            value = (applied - center_shift * own[layer, q]) * (1.0 / half_range)
            if not first:
                value = 2.0 * value - before[layer, q]
            out[layer, q] = value
    if not last:
        refs[1][0] = out[even * (layers - 1)]
        refs[2][0] = out[(1 - even) * (layers - 1)]


def step(packed, cols, info, own, other, edges, before, last):
    layers, cross_local, size, columns = own.shape
    rows, _, depth = packed.shape
    whole = pl.BlockSpec(memory_space=pltpu.VMEM)
    scalar = pl.BlockSpec(memory_space=pltpu.SMEM)
    args = [packed, own, other, *edges] + ([] if before is None else [before])
    edge = jax.ShapeDtypeStruct((1,) + own.shape[1:], jnp.float32)
    shapes = [jax.ShapeDtypeStruct(own.shape, jnp.float32)] + ([] if last else [edge, edge])
    return pl.pallas_call(
        functools.partial(step_kernel, before is None, last, cols.shape[2]),
        in_specs=[scalar, scalar] + [whole] * len(args),
        out_specs=[whole] * len(shapes),
        out_shape=shapes,
        scratch_shapes=[
            pltpu.VMEM(((layers + 2) * 2 * cross_local, size, 2 * columns), jnp.bfloat16)
        ],
        cost_estimate=estimate(1.7),
        compiler_params=pltpu.CompilerParams(vmem_limit_bytes=VMEM_LIMIT),
        name="step",
    )(info, cols, *args)


def gram_kernel(pairs, info, *refs):
    *powers, mine, theirs, block, held = refs
    columns = mine.shape[1]
    half = columns // 2
    for j, power in enumerate(powers):
        high, low = split(power[...].reshape(-1, columns))
        held[j, :, :columns] = high
        held[j, :, columns:] = low
    for place, (i, j) in enumerate(pairs):
        acc = lax.dot_general(
            held[i], held[j], (((0,), (0,)), ((), ())), preferred_element_type=jnp.float32
        )
        acc = acc[:, :columns] + acc[:, columns:]
        block[place] = acc[:columns] + acc[columns:]
        for core, out in ((info[0], mine), (1 - info[0], theirs)):
            rows = pl.ds(pl.multiple_of(core * half, half), half)
            out[place * half : (place + 1) * half, :] = block[place, rows, :]
    used = len(pairs) * half
    if used < mine.shape[0]:
        for out in (mine, theirs):
            out[used:, :] = jnp.zeros((mine.shape[0] - used, columns), jnp.float32)


def gram_blocks(powers, pairs, info, count):
    columns = powers[0].shape[-1]
    rows = powers[0].size // columns
    whole = pl.BlockSpec(memory_space=pltpu.VMEM)
    tall = share(len(pairs), columns, count) * count
    return pl.pallas_call(
        functools.partial(gram_kernel, pairs),
        in_specs=[pl.BlockSpec(memory_space=pltpu.SMEM)] + [whole] * len(powers),
        out_specs=[whole] * 2,
        out_shape=[jax.ShapeDtypeStruct((tall, columns), jnp.float32)] * 2,
        scratch_shapes=[
            pltpu.VMEM((len(pairs), columns, columns), jnp.float32),
            pltpu.VMEM((len(powers), rows, 2 * columns), jnp.bfloat16),
        ],
        cost_estimate=estimate(1.4),
        compiler_params=pltpu.CompilerParams(vmem_limit_bytes=VMEM_LIMIT),
        name="gram",
    )(info, *powers)


def share(blocks, columns, count):
    return -(-blocks * (columns // 2) // count)


def factor(block):
    size = block.shape[0]
    tall = 8
    tiles = size // tall
    lanes = lax.broadcasted_iota(jnp.int32, (tall, size), 1)
    sub = lax.broadcasted_iota(jnp.int32, (tall, size), 0)
    gram = [block[tall * t : tall * (t + 1)] for t in range(tiles)]
    unit = [jnp.where(lanes == sub + tall * t, 1.0, 0.0) for t in range(tiles)]

    def spread(x, row):
        return jnp.broadcast_to(x[row : row + 1], (tall, size))

    def lane(x, at):
        return jnp.broadcast_to(x[:, at : at + 1], (tall, size))

    corner = [lane(gram[0], c) for c in range(tall)]
    for p in range(tiles):
        at = tall * p
        below = range(p + 1, tiles)
        cols = [[lane(gram[t], at + c) for t in below] for c in range(tall)]
        ahead = [lane(gram[p + 1], at + tall + d) for d in range(tall)] if p + 1 < tiles else []
        scales, tops, lows = [], [], []
        for c in range(tall):
            scale = lax.rsqrt(spread(corner[c], c))
            square = scale * scale
            top = jnp.where(sub > c, corner[c], 0.0)
            weights = [spread(corner[d], c) for d in range(c + 1, tall)]
            for d in range(c + 1, tall):
                corner[d] = corner[d] - (top * weights[d - c - 1]) * square
            low = [x * scale for x in cols[c]]
            for d in range(c + 1, tall):
                weight = weights[d - c - 1] * scale
                cols[d] = [x - m * weight for x, m in zip(cols[d], low)]
            if low:
                ahead = [x - low[0] * spread(low[0], d) for d, x in enumerate(ahead)]
            scales.append(scale)
            tops.append(top * scale)
            lows.append(low)
        for c in range(tall):
            row_gram = spread(gram[p], c) * scales[c]
            row_unit = spread(unit[p], c) * scales[c]
            gram[p] = jnp.where(sub == c, row_gram, gram[p] - tops[c] * row_gram)
            unit[p] = jnp.where(sub == c, row_unit, unit[p] - tops[c] * row_unit)
            for t, m in zip(below, lows[c]):
                gram[t] = gram[t] - m * row_gram
                unit[t] = unit[t] - m * row_unit
        corner = ahead
    upper = [jnp.where(lanes >= sub + tall * t, gram[t], 0.0) for t in range(tiles)]
    return jnp.concatenate(upper, axis=0), jnp.concatenate(unit, axis=0)


def dot(a, b, right=0):
    (a_high, a_low), (b_high, b_low) = split(a), split(b)

    def product(x, y):
        return lax.dot_general(
            x, y, (((1,), (right,)), ((), ())), preferred_element_type=jnp.float32
        )

    return product(a_high, b_high) + (product(a_high, b_low) + product(a_low, b_high))


def column_kernel(place, first, scale, info, own, other, *refs):
    *refs, upper_out, inverse_out, gram = refs
    size = gram.shape[0]
    half = size // 2
    at = place * size
    for core, source in ((info[0], own), (1 - info[0], other)):
        rows = pl.ds(pl.multiple_of(core * half, half), half)
        for j in range(place + 1):
            gram[rows, j * size : (j + 1) * size] = source[(first + j) * half : (first + j + 1) * half, :]
    corner = gram[:, at:]
    if place:
        known, upper_known = refs
        left = dot(gram[:, :at], known[...], 1)
        corner = corner - dot(left, left, 1)
        carried = dot(left, known[...])
    upper, inverse = factor(corner)
    if place:
        inverse_out[at:, :at] = -dot(inverse, carried)
        inverse_out[:at, :at] = known[...]
        inverse_out[:at, at:] = jnp.zeros((at, size), jnp.float32)
        upper_out[:at, :at] = upper_known[...] * scale
        upper_out[at:, :at] = jnp.zeros((size, at), jnp.float32)
        upper_out[:at, at:] = left.T * scale
    inverse_out[at:, at:] = inverse
    upper_out[at:, at:] = upper * scale


def column(place, first, info, own, other, before, scale=1.0):
    whole = pl.BlockSpec(memory_space=pltpu.VMEM)
    size = own.shape[1]
    args = [own, other, *before]
    square = jax.ShapeDtypeStruct(((place + 1) * size,) * 2, jnp.float32)
    return pl.pallas_call(
        functools.partial(column_kernel, place, first, scale),
        in_specs=[pl.BlockSpec(memory_space=pltpu.SMEM)] + [whole] * len(args),
        out_specs=[whole, whole],
        out_shape=[square, square],
        scratch_shapes=[pltpu.VMEM((size, (place + 1) * size), jnp.float32)],
        compiler_params=pltpu.CompilerParams(vmem_limit_bytes=VMEM_LIMIT),
        cost_estimate=estimate(4.0),
        name="column",
    )(info, *args)


def basis_kernel(scale, count, *refs):
    *powers, inverse, out, high, low = refs
    columns = powers[0].shape[-1]

    @pl.when(pl.program_id(0) == 0)
    def _():
        high[...], low[...] = split(inverse[...] * scale)

    pairs = [split(p[...].reshape(-1, columns)) for p in powers]
    wide = 2 * columns
    for start in range(0, count * columns, wide):
        stop = min(start + wide, count * columns)
        left_high = jnp.concatenate([p[0] for p in pairs[: stop // columns]], axis=1)
        left_low = jnp.concatenate([p[1] for p in pairs[: stop // columns]], axis=1)
        acc = None
        for left, right in ((left_high, high), (left_low, high), (left_high, low)):
            term = lax.dot_general(
                left,
                right[start:stop, :stop],
                (((1,), (1,)), ((), ())),
                preferred_element_type=jnp.float32,
            )
            acc = term if acc is None else acc + term
        out[:, :, :, start:stop] = acc.astype(jnp.bfloat16).reshape(out.shape[:3] + (stop - start,))


def basis_of(powers, inverse, scale):
    layers, cross_local, size, columns = powers[0].shape
    count = len(powers)
    full = count * columns
    return pl.pallas_call(
        functools.partial(basis_kernel, scale, count),
        grid=(layers,),
        in_specs=[pl.BlockSpec((1, cross_local, size, columns), lambda i: (i, 0, 0, 0))] * count
        + [pl.BlockSpec(inverse.shape, lambda i: (0, 0))],
        out_specs=pl.BlockSpec((1, cross_local, size, full), lambda i: (i, 0, 0, 0)),
        out_shape=jax.ShapeDtypeStruct((layers, cross_local, size, full), jnp.bfloat16),
        scratch_shapes=[pltpu.VMEM((full, full), jnp.bfloat16)] * 2,
        compiler_params=pltpu.CompilerParams(vmem_limit_bytes=VMEM_LIMIT),
        cost_estimate=estimate(3.0),
        name="basis",
    )(*powers, inverse)


def local(sources, couplings, block_cols, lead_sites, lead_sigma):
    layers, cross_local, size, columns = sources.shape
    cross_count = lax.axis_size("cross")
    count = lax.axis_size("trans")
    place = lax.axis_index("trans")
    even = 1 - place % 2
    info = jnp.stack([lax.axis_index("cross"), place == 0, place == count - 1, even])
    info = jnp.concatenate([info.astype(jnp.int32), lead_sites])
    packed = pack(couplings, lead_sigma, info)
    scale_rows = math.sqrt(count * layers * cross_local * cross_count * size)

    near = [(i, i ^ 1) for i in range(count) if i ^ 1 < count]
    far = [(i, j) for i in range(count) for j in (i - 1 + 2 * (i % 2),) if 0 <= j < count]

    def swap(x):
        return lax.ppermute(x, "cross", [(0, 1), (1, 0)])

    def exchange(x):
        return lax.all_to_all(x, "trans", 0, 0, tiled=True)

    early = tuple((i, j) for i in range(S) for j in range(i + 1))
    powers = [sources]
    near_layer = lax.dynamic_slice_in_dim(sources, even * (layers - 1), 1)
    far_layer = lax.dynamic_slice_in_dim(sources, (1 - even) * (layers - 1), 1)
    for k in range(S):
        field = powers[k]
        far_edge = lax.ppermute(far_layer, "trans", far)
        near_edge = lax.ppermute(near_layer, "trans", near)
        other = swap(field)
        if k == 0:
            near_edge, far_edge, packed = lax.optimization_barrier((near_edge, far_edge, packed))
        if k == S - 1:
            mine, theirs = gram_blocks(powers, early, info, count)
            shares = (mine + swap(theirs)).reshape(count, -1, columns)
            near_edge, far_edge, shares = lax.optimization_barrier((near_edge, far_edge, shares))
            parts = exchange(shares)
        edges = (near_edge, swap(near_edge), far_edge, swap(far_edge))
        before = powers[k - 1] if k else None
        got = step(packed, block_cols, info, field, other, edges, before, k == S - 1)
        powers.append(got[0])
        if k < S - 1:
            near_layer, far_layer = got[1:]
    mine, theirs = gram_blocks(powers, tuple((S, j) for j in range(S + 1)), info, count)
    last = mine + swap(theirs)
    last, parts = lax.optimization_barrier((last, parts))
    summed = jnp.sum(parts, axis=0, keepdims=True)
    known = exchange(jnp.broadcast_to(summed, parts.shape)).reshape(-1, columns)
    known_other = swap(known)
    reach = 1
    while reach < count:
        last = last + lax.ppermute(last, "trans", [(i, i ^ reach) for i in range(count)])
        reach *= 2
    first = column(0, 0, info, known, known_other, ())
    second = column(1, 1, info, known, known_other, first[::-1])
    third = column(2, 3, info, known, known_other, second[::-1])
    r_factor, inverse = column(3, 0, info, last, swap(last), third[::-1], 1.0 / scale_rows)
    return basis_of(powers, inverse, scale_rows), r_factor


def solution(mesh):
    return jax.shard_map(
        local,
        mesh=mesh,
        in_specs=(
            P(("energy", "trans"), "cross", None, None),
            P(("energy", "trans"), "cross", None, None, None),
            P("trans", "cross", None),
            P(),
            P("energy", None, None),
        ),
        out_specs=(P(("energy", "trans"), "cross", None, None), P("energy", None)),
        check_vma=False,
    )
```

```python
import functools
import math

import jax
import jax.numpy as jnp
from jax import lax
from jax.experimental import pallas as pl
from jax.experimental.pallas import tpu as pltpu
from jax.sharding import PartitionSpec as P

S = 3
center_shift = 2.0
half_range = 1.6
VMEM_LIMIT = 16 * 1024 * 1024


def estimate(us):
    return pl.CostEstimate(flops=int(us * 1.15e9), bytes_accessed=0, transcendentals=0)


def split(x):
    high = x.astype(jnp.bfloat16)
    low = (x - high.astype(jnp.float32)).astype(jnp.bfloat16)
    return high, low


def pack_kernel(info, sites, held, leads, out):
    layers, cross_local, slots, size, _ = held.shape
    contacts = leads.shape[0]
    for layer in range(layers):
        for q in range(cross_local):
            place = info[0] * cross_local + q
            lead = jnp.zeros((size, size), jnp.float32)
            for k in range(contacts):
                end, flag = (0, info[1]) if k < contacts // 2 else (layers - 1, info[2])
                if layer == end:
                    here = jnp.logical_and(flag == 1, sites[k] == place)
                    lead = lead - leads[k] * jnp.where(here, 1.0, 0.0)
            blocks = [held[layer, q, j] for j in range(slots)] + [lead]
            row = jnp.concatenate(
                [jnp.concatenate(blocks[i : i + 2], axis=1) for i in range(0, slots + 1, 2)],
                axis=1,
            )
            high, low = split(row)
            out[layer * cross_local + q, :size] = high
            out[layer * cross_local + q, size:] = low


def pack(couplings, lead_sites, lead_sigma, info):
    layers, cross_local, slots, size, _ = couplings.shape
    scalar = pl.BlockSpec(memory_space=pltpu.SMEM)
    whole = pl.BlockSpec(memory_space=pltpu.VMEM)
    return pl.pallas_call(
        pack_kernel,
        in_specs=[scalar, scalar, whole, whole],
        out_specs=whole,
        out_shape=jax.ShapeDtypeStruct(
            (layers * cross_local, 2 * size, (slots + 1) * size), jnp.bfloat16
        ),
        compiler_params=pltpu.CompilerParams(vmem_limit_bytes=VMEM_LIMIT),
        cost_estimate=estimate(2.5),
        name="pack",
    )(info, lead_sites, couplings, lead_sigma)


def step_kernel(first, last, slots, info, cols, packed, own, other, *refs):
    edges, refs = refs[:4], refs[4:]
    before, refs = (None, refs) if first else (refs[0], refs[1:])
    out, field = refs[0], refs[-1]
    layers, cross_local, size, columns = own.shape
    total = 2 * cross_local
    mine = info[0] * cross_local
    theirs = (1 - info[0]) * cross_local

    def put(place, x):
        high, low = split(x)
        field[place, :, :columns] = high
        field[place, :, columns:] = low

    for layer in range(layers):
        for q in range(cross_local):
            put((layer + 1) * total + mine + q, own[layer, q])
            put((layer + 1) * total + theirs + q, other[layer, q])
    even = info[3]
    for pair, place in enumerate((1 - even, even)):
        for q in range(cross_local):
            put(place * (layers + 1) * total + mine + q, edges[2 * pair][0, q])
            put(place * (layers + 1) * total + theirs + q, edges[2 * pair + 1][0, q])
    for layer in range(layers):
        for q in range(cross_local):
            row = layer * cross_local + q
            places = [cols[layer, q, j] for j in range(slots)] + [total + mine + q]
            picked = jnp.concatenate([field[layer * total + c] for c in places], axis=0)
            acc = jnp.dot(packed[row], picked, preferred_element_type=jnp.float32)
            acc = acc[:, :columns] + acc[:, columns:]
            applied = acc[:size] + acc[size:]
            value = (applied - center_shift * own[layer, q]) * (1.0 / half_range)
            if not first:
                value = 2.0 * value - before[layer, q]
            out[layer, q] = value
    if not last:
        refs[1][0] = out[even * (layers - 1)]
        refs[2][0] = out[(1 - even) * (layers - 1)]


def step(packed, cols, info, own, other, edges, before, last):
    layers, cross_local, size, columns = own.shape
    rows, _, depth = packed.shape
    whole = pl.BlockSpec(memory_space=pltpu.VMEM)
    scalar = pl.BlockSpec(memory_space=pltpu.SMEM)
    args = [packed, own, other, *edges] + ([] if before is None else [before])
    edge = jax.ShapeDtypeStruct((1,) + own.shape[1:], jnp.float32)
    shapes = [jax.ShapeDtypeStruct(own.shape, jnp.float32)] + ([] if last else [edge, edge])
    return pl.pallas_call(
        functools.partial(step_kernel, before is None, last, cols.shape[2]),
        in_specs=[scalar, scalar] + [whole] * len(args),
        out_specs=[whole] * len(shapes),
        out_shape=shapes,
        scratch_shapes=[
            pltpu.VMEM(((layers + 2) * 2 * cross_local, size, 2 * columns), jnp.bfloat16)
        ],
        cost_estimate=estimate(1.7),
        compiler_params=pltpu.CompilerParams(vmem_limit_bytes=VMEM_LIMIT),
        name="step",
    )(info, cols, *args)


def gram_kernel(pairs, info, *refs):
    *powers, mine, theirs, block, held = refs
    columns = mine.shape[1]
    half = columns // 2
    for j, power in enumerate(powers):
        high, low = split(power[...].reshape(-1, columns))
        held[j, :, :columns] = high
        held[j, :, columns:] = low
    for place, (i, j) in enumerate(pairs):
        acc = lax.dot_general(
            held[i], held[j], (((0,), (0,)), ((), ())), preferred_element_type=jnp.float32
        )
        acc = acc[:, :columns] + acc[:, columns:]
        block[place] = acc[:columns] + acc[columns:]
        for core, out in ((info[0], mine), (1 - info[0], theirs)):
            rows = pl.ds(pl.multiple_of(core * half, half), half)
            out[place * half : (place + 1) * half, :] = block[place, rows, :]
    used = len(pairs) * half
    if used < mine.shape[0]:
        for out in (mine, theirs):
            out[used:, :] = jnp.zeros((mine.shape[0] - used, columns), jnp.float32)


def gram_blocks(powers, pairs, info, count):
    columns = powers[0].shape[-1]
    rows = powers[0].size // columns
    whole = pl.BlockSpec(memory_space=pltpu.VMEM)
    tall = share(len(pairs), columns, count) * count
    return pl.pallas_call(
        functools.partial(gram_kernel, pairs),
        in_specs=[pl.BlockSpec(memory_space=pltpu.SMEM)] + [whole] * len(powers),
        out_specs=[whole] * 2,
        out_shape=[jax.ShapeDtypeStruct((tall, columns), jnp.float32)] * 2,
        scratch_shapes=[
            pltpu.VMEM((len(pairs), columns, columns), jnp.float32),
            pltpu.VMEM((len(powers), rows, 2 * columns), jnp.bfloat16),
        ],
        cost_estimate=estimate(1.4),
        compiler_params=pltpu.CompilerParams(vmem_limit_bytes=VMEM_LIMIT),
        name="gram",
    )(info, *powers)


def share(blocks, columns, count):
    return -(-blocks * (columns // 2) // count)


def factor(block):
    size = block.shape[0]
    tall = 8
    tiles = size // tall
    lanes = lax.broadcasted_iota(jnp.int32, (tall, size), 1)
    sub = lax.broadcasted_iota(jnp.int32, (tall, size), 0)
    gram = [block[tall * t : tall * (t + 1)] for t in range(tiles)]
    unit = [jnp.where(lanes == sub + tall * t, 1.0, 0.0) for t in range(tiles)]

    def spread(x, row):
        return jnp.broadcast_to(x[row : row + 1], (tall, size))

    def lane(x, at):
        return jnp.broadcast_to(x[:, at : at + 1], (tall, size))

    corner = [lane(gram[0], c) for c in range(tall)]
    for p in range(tiles):
        at = tall * p
        below = range(p + 1, tiles)
        cols = [[lane(gram[t], at + c) for t in below] for c in range(tall)]
        ahead = [lane(gram[p + 1], at + tall + d) for d in range(tall)] if p + 1 < tiles else []
        scales, tops, lows = [], [], []
        for c in range(tall):
            scale = lax.rsqrt(spread(corner[c], c))
            square = scale * scale
            top = jnp.where(sub > c, corner[c], 0.0)
            weights = [spread(corner[d], c) for d in range(c + 1, tall)]
            for d in range(c + 1, tall):
                corner[d] = corner[d] - (top * weights[d - c - 1]) * square
            low = [x * scale for x in cols[c]]
            for d in range(c + 1, tall):
                weight = weights[d - c - 1] * scale
                cols[d] = [x - m * weight for x, m in zip(cols[d], low)]
            if low:
                ahead = [x - low[0] * spread(low[0], d) for d, x in enumerate(ahead)]
            scales.append(scale)
            tops.append(top * scale)
            lows.append(low)
        for c in range(tall):
            row_gram = spread(gram[p], c) * scales[c]
            row_unit = spread(unit[p], c) * scales[c]
            gram[p] = jnp.where(sub == c, row_gram, gram[p] - tops[c] * row_gram)
            unit[p] = jnp.where(sub == c, row_unit, unit[p] - tops[c] * row_unit)
            for t, m in zip(below, lows[c]):
                gram[t] = gram[t] - m * row_gram
                unit[t] = unit[t] - m * row_unit
        corner = ahead
    upper = [jnp.where(lanes >= sub + tall * t, gram[t], 0.0) for t in range(tiles)]
    return jnp.concatenate(upper, axis=0), jnp.concatenate(unit, axis=0)


def dot(a, b, right=0):
    (a_high, a_low), (b_high, b_low) = split(a), split(b)

    def product(x, y):
        return lax.dot_general(
            x, y, (((1,), (right,)), ((), ())), preferred_element_type=jnp.float32
        )

    return product(a_high, b_high) + (product(a_high, b_low) + product(a_low, b_high))


def column_kernel(place, first, scale, info, own, other, *refs):
    *refs, upper_out, inverse_out, gram = refs
    size = gram.shape[0]
    half = size // 2
    at = place * size
    for core, source in ((info[0], own), (1 - info[0], other)):
        rows = pl.ds(pl.multiple_of(core * half, half), half)
        for j in range(place + 1):
            gram[rows, j * size : (j + 1) * size] = source[(first + j) * half : (first + j + 1) * half, :]
    corner = gram[:, at:]
    if place:
        known, upper_known = refs
        left = dot(gram[:, :at], known[...], 1)
        corner = corner - dot(left, left, 1)
        carried = dot(left, known[...])
    upper, inverse = factor(corner)
    if place:
        inverse_out[at:, :at] = -dot(inverse, carried)
        inverse_out[:at, :at] = known[...]
        inverse_out[:at, at:] = jnp.zeros((at, size), jnp.float32)
        upper_out[:at, :at] = upper_known[...] * scale
        upper_out[at:, :at] = jnp.zeros((size, at), jnp.float32)
        upper_out[:at, at:] = left.T * scale
    inverse_out[at:, at:] = inverse
    upper_out[at:, at:] = upper * scale


def column(place, first, info, own, other, before, scale=1.0):
    whole = pl.BlockSpec(memory_space=pltpu.VMEM)
    size = own.shape[1]
    args = [own, other, *before]
    square = jax.ShapeDtypeStruct(((place + 1) * size,) * 2, jnp.float32)
    return pl.pallas_call(
        functools.partial(column_kernel, place, first, scale),
        in_specs=[pl.BlockSpec(memory_space=pltpu.SMEM)] + [whole] * len(args),
        out_specs=[whole, whole],
        out_shape=[square, square],
        scratch_shapes=[pltpu.VMEM((size, (place + 1) * size), jnp.float32)],
        compiler_params=pltpu.CompilerParams(vmem_limit_bytes=VMEM_LIMIT),
        cost_estimate=estimate(4.0),
        name="column",
    )(info, *args)


def basis_kernel(scale, count, *refs):
    *powers, inverse, out, high, low = refs
    columns = powers[0].shape[-1]

    @pl.when(pl.program_id(0) == 0)
    def _():
        high[...], low[...] = split(inverse[...] * scale)

    pairs = [split(p[...].reshape(-1, columns)) for p in powers]
    wide = 2 * columns
    for start in range(0, count * columns, wide):
        stop = min(start + wide, count * columns)
        left_high = jnp.concatenate([p[0] for p in pairs[: stop // columns]], axis=1)
        left_low = jnp.concatenate([p[1] for p in pairs[: stop // columns]], axis=1)
        acc = None
        for left, right in ((left_high, high), (left_low, high), (left_high, low)):
            term = lax.dot_general(
                left,
                right[start:stop, :stop],
                (((1,), (1,)), ((), ())),
                preferred_element_type=jnp.float32,
            )
            acc = term if acc is None else acc + term
        out[:, :, :, start:stop] = acc.astype(jnp.bfloat16).reshape(out.shape[:3] + (stop - start,))


def basis_of(powers, inverse, scale):
    layers, cross_local, size, columns = powers[0].shape
    count = len(powers)
    full = count * columns
    return pl.pallas_call(
        functools.partial(basis_kernel, scale, count),
        grid=(layers,),
        in_specs=[pl.BlockSpec((1, cross_local, size, columns), lambda i: (i, 0, 0, 0))] * count
        + [pl.BlockSpec(inverse.shape, lambda i: (0, 0))],
        out_specs=pl.BlockSpec((1, cross_local, size, full), lambda i: (i, 0, 0, 0)),
        out_shape=jax.ShapeDtypeStruct((layers, cross_local, size, full), jnp.bfloat16),
        scratch_shapes=[pltpu.VMEM((full, full), jnp.bfloat16)] * 2,
        compiler_params=pltpu.CompilerParams(vmem_limit_bytes=VMEM_LIMIT),
        cost_estimate=estimate(3.0),
        name="basis",
    )(*powers, inverse)


def local(sources, couplings, block_cols, lead_sites, lead_sigma):
    layers, cross_local, size, columns = sources.shape
    cross_count = lax.axis_size("cross")
    count = lax.axis_size("trans")
    place = lax.axis_index("trans")
    even = 1 - place % 2
    info = jnp.stack([lax.axis_index("cross"), place == 0, place == count - 1, even])
    info = info.astype(jnp.int32)
    packed = pack(couplings, lead_sites, lead_sigma, info)
    scale_rows = math.sqrt(count * layers * cross_local * cross_count * size)

    near = [(i, i ^ 1) for i in range(count) if i ^ 1 < count]
    far = [(i, j) for i in range(count) for j in (i - 1 + 2 * (i % 2),) if 0 <= j < count]

    def swap(x):
        return lax.ppermute(x, "cross", [(0, 1), (1, 0)])

    def exchange(x):
        return lax.all_to_all(x, "trans", 0, 0, tiled=True)

    def double(x, reach):
        return x + lax.ppermute(x, "trans", [(i, i ^ reach) for i in range(count)])

    early = tuple((i, j) for i in range(S) for j in range(i + 1))
    powers = [sources]
    near_layer = lax.dynamic_slice_in_dim(sources, even * (layers - 1), 1)
    far_layer = lax.dynamic_slice_in_dim(sources, (1 - even) * (layers - 1), 1)
    for k in range(S):
        field = powers[k]
        far_edge = lax.ppermute(far_layer, "trans", far)
        near_edge = lax.ppermute(near_layer, "trans", near)
        other = swap(field)
        if k == 0:
            near_edge, far_edge, packed = lax.optimization_barrier((near_edge, far_edge, packed))
        if k == S - 1:
            held, other = lax.optimization_barrier((field, other))
            mine, theirs = gram_blocks([*powers[:-1], held], early, info, count)
            shares = (mine + swap(theirs)).reshape(count, -1, columns)
            near_edge, far_edge, shares = lax.optimization_barrier((near_edge, far_edge, shares))
            parts = exchange(shares)
        edges = (far_edge, swap(far_edge), near_edge, swap(near_edge))
        before = powers[k - 1] if k else None
        got = step(packed, block_cols, info, field, other, edges, before, k == S - 1)
        powers.append(got[0])
        if k < S - 1:
            near_layer, far_layer = got[1:]
    mine, theirs = gram_blocks(powers, tuple((S, j) for j in range(S + 1)), info, count)
    last = mine + swap(theirs)
    last, parts = lax.optimization_barrier((last, parts))
    summed = jnp.sum(parts, axis=0, keepdims=True)
    known = exchange(jnp.broadcast_to(summed, parts.shape)).reshape(-1, columns)
    known_other = swap(known)
    first = column(0, 0, info, known, known_other, ())
    reach = 1
    while reach < count:
        last = double(last, reach)
        reach *= 2
        if reach == count // 2:
            last, first = lax.optimization_barrier((last, first))
    second = column(1, 1, info, known, known_other, first[::-1])
    last, second = lax.optimization_barrier((last, second))
    third = column(2, 3, info, known, known_other, second[::-1])
    r_factor, inverse = column(3, 0, info, last, swap(last), third[::-1], 1.0 / scale_rows)
    return basis_of(powers, inverse, scale_rows), r_factor


def solution(mesh):
    return jax.shard_map(
        local,
        mesh=mesh,
        in_specs=(
            P(("energy", "trans"), "cross", None, None),
            P(("energy", "trans"), "cross", None, None, None),
            P("trans", "cross", None),
            P(),
            P("energy", None, None),
        ),
        out_specs=(P(("energy", "trans"), "cross", None, None), P("energy", None)),
        check_vma=False,
    )
```

```python
import functools
import math

import jax
import jax.numpy as jnp
from jax import lax
from jax.experimental import pallas as pl
from jax.experimental.pallas import tpu as pltpu
from jax.sharding import PartitionSpec as P

S = 3
center_shift = 2.0
half_range = 1.6
VMEM_LIMIT = 16 * 1024 * 1024


def estimate(us):
    return pl.CostEstimate(flops=int(us * 1.15e9), bytes_accessed=0, transcendentals=0)


def split(x):
    high = x.astype(jnp.bfloat16)
    low = (x - high.astype(jnp.float32)).astype(jnp.bfloat16)
    return high, low


def pack_kernel(info, sites, held, leads, out):
    layers, cross_local, slots, size, _ = held.shape
    contacts = leads.shape[0]
    for layer in range(layers):
        for q in range(cross_local):
            place = info[0] * cross_local + q
            lead = jnp.zeros((size, size), jnp.float32)
            for k in range(contacts):
                end, flag = (0, info[1]) if k < contacts // 2 else (layers - 1, info[2])
                if layer == end:
                    here = jnp.logical_and(flag == 1, sites[k] == place)
                    lead = lead - leads[k] * jnp.where(here, 1.0, 0.0)
            blocks = [held[layer, q, j] for j in range(slots)] + [lead]
            row = jnp.concatenate(
                [jnp.concatenate(blocks[i : i + 2], axis=1) for i in range(0, slots + 1, 2)],
                axis=1,
            )
            high, low = split(row)
            out[layer * cross_local + q, :size] = high
            out[layer * cross_local + q, size:] = low


def pack(couplings, lead_sites, lead_sigma, info):
    layers, cross_local, slots, size, _ = couplings.shape
    scalar = pl.BlockSpec(memory_space=pltpu.SMEM)
    whole = pl.BlockSpec(memory_space=pltpu.VMEM)
    return pl.pallas_call(
        pack_kernel,
        in_specs=[scalar, scalar, whole, whole],
        out_specs=whole,
        out_shape=jax.ShapeDtypeStruct(
            (layers * cross_local, 2 * size, (slots + 1) * size), jnp.bfloat16
        ),
        compiler_params=pltpu.CompilerParams(vmem_limit_bytes=VMEM_LIMIT),
        cost_estimate=estimate(2.5),
        name="pack",
    )(info, lead_sites, couplings, lead_sigma)


def step_kernel(first, last, slots, info, cols, packed, own, other, *refs):
    edges, refs = refs[:4], refs[4:]
    before, refs = (None, refs) if first else (refs[0], refs[1:])
    out, field = refs[0], refs[-1]
    layers, cross_local, size, columns = own.shape
    total = 2 * cross_local
    mine = info[0] * cross_local
    theirs = (1 - info[0]) * cross_local

    def put(place, x):
        high, low = split(x)
        field[place, :, :columns] = high
        field[place, :, columns:] = low

    for layer in range(layers):
        for q in range(cross_local):
            put((layer + 1) * total + mine + q, own[layer, q])
            put((layer + 1) * total + theirs + q, other[layer, q])
    even = info[3]
    for pair, place in enumerate((even, 1 - even)):
        for q in range(cross_local):
            put(place * (layers + 1) * total + mine + q, edges[2 * pair][0, q])
            put(place * (layers + 1) * total + theirs + q, edges[2 * pair + 1][0, q])
    for layer in range(layers):
        for q in range(cross_local):
            row = layer * cross_local + q
            places = [cols[layer, q, j] for j in range(slots)] + [total + mine + q]
            picked = jnp.concatenate([field[layer * total + c] for c in places], axis=0)
            acc = jnp.dot(packed[row], picked, preferred_element_type=jnp.float32)
            acc = acc[:, :columns] + acc[:, columns:]
            applied = acc[:size] + acc[size:]
            value = (applied - center_shift * own[layer, q]) * (1.0 / half_range)
            if not first:
                value = 2.0 * value - before[layer, q]
            out[layer, q] = value
    if not last:
        refs[1][0] = out[even * (layers - 1)]
        refs[2][0] = out[(1 - even) * (layers - 1)]


def step(packed, cols, info, own, other, edges, before, last):
    layers, cross_local, size, columns = own.shape
    rows, _, depth = packed.shape
    whole = pl.BlockSpec(memory_space=pltpu.VMEM)
    scalar = pl.BlockSpec(memory_space=pltpu.SMEM)
    args = [packed, own, other, *edges] + ([] if before is None else [before])
    edge = jax.ShapeDtypeStruct((1,) + own.shape[1:], jnp.float32)
    shapes = [jax.ShapeDtypeStruct(own.shape, jnp.float32)] + ([] if last else [edge, edge])
    return pl.pallas_call(
        functools.partial(step_kernel, before is None, last, cols.shape[2]),
        in_specs=[scalar, scalar] + [whole] * len(args),
        out_specs=[whole] * len(shapes),
        out_shape=shapes,
        scratch_shapes=[
            pltpu.VMEM(((layers + 2) * 2 * cross_local, size, 2 * columns), jnp.bfloat16)
        ],
        cost_estimate=estimate(1.7),
        compiler_params=pltpu.CompilerParams(vmem_limit_bytes=VMEM_LIMIT),
        name="step",
    )(info, cols, *args)


def gram_kernel(pairs, info, *refs):
    *powers, mine, theirs, block, held = refs
    columns = mine.shape[1]
    half = columns // 2
    for j, power in enumerate(powers):
        high, low = split(power[...].reshape(-1, columns))
        held[j, :, :columns] = high
        held[j, :, columns:] = low
    for place, (i, j) in enumerate(pairs):
        acc = lax.dot_general(
            held[i], held[j], (((0,), (0,)), ((), ())), preferred_element_type=jnp.float32
        )
        acc = acc[:, :columns] + acc[:, columns:]
        block[place] = acc[:columns] + acc[columns:]
        for core, out in ((info[0], mine), (1 - info[0], theirs)):
            rows = pl.ds(pl.multiple_of(core * half, half), half)
            out[place * half : (place + 1) * half, :] = block[place, rows, :]
    used = len(pairs) * half
    if used < mine.shape[0]:
        for out in (mine, theirs):
            out[used:, :] = jnp.zeros((mine.shape[0] - used, columns), jnp.float32)


def gram_blocks(powers, pairs, info, count):
    columns = powers[0].shape[-1]
    rows = powers[0].size // columns
    whole = pl.BlockSpec(memory_space=pltpu.VMEM)
    tall = share(len(pairs), columns, count) * count
    return pl.pallas_call(
        functools.partial(gram_kernel, pairs),
        in_specs=[pl.BlockSpec(memory_space=pltpu.SMEM)] + [whole] * len(powers),
        out_specs=[whole] * 2,
        out_shape=[jax.ShapeDtypeStruct((tall, columns), jnp.float32)] * 2,
        scratch_shapes=[
            pltpu.VMEM((len(pairs), columns, columns), jnp.float32),
            pltpu.VMEM((len(powers), rows, 2 * columns), jnp.bfloat16),
        ],
        cost_estimate=estimate(1.4),
        compiler_params=pltpu.CompilerParams(vmem_limit_bytes=VMEM_LIMIT),
        name="gram",
    )(info, *powers)


def share(blocks, columns, count):
    return -(-blocks * (columns // 2) // count)


def factor(block):
    size = block.shape[0]
    tall = 8
    tiles = size // tall
    lanes = lax.broadcasted_iota(jnp.int32, (tall, size), 1)
    sub = lax.broadcasted_iota(jnp.int32, (tall, size), 0)
    gram = [block[tall * t : tall * (t + 1)] for t in range(tiles)]
    unit = [jnp.where(lanes == sub + tall * t, 1.0, 0.0) for t in range(tiles)]

    def spread(x, row):
        return jnp.broadcast_to(x[row : row + 1], (tall, size))

    def lane(x, at):
        return jnp.broadcast_to(x[:, at : at + 1], (tall, size))

    corner = [lane(gram[0], c) for c in range(tall)]
    for p in range(tiles):
        at = tall * p
        more = p + 1 < tiles
        cols = [lane(gram[p + 1], at + c) for c in range(tall)] if more else []
        ahead = [lane(gram[p + 1], at + tall + d) for d in range(tall)] if more else []
        scales, tops = [], []
        for c in range(tall):
            scale = lax.rsqrt(spread(corner[c], c))
            square = scale * scale
            top = jnp.where(sub > c, corner[c], 0.0)
            weights = [spread(corner[d], c) for d in range(c + 1, tall)]
            for d in range(c + 1, tall):
                corner[d] = corner[d] - (top * weights[d - c - 1]) * square
            if more:
                low = cols[c] * scale
                for d in range(c + 1, tall):
                    cols[d] = cols[d] - low * (weights[d - c - 1] * scale)
                ahead = [x - low * spread(low, d) for d, x in enumerate(ahead)]
            scales.append(scale)
            tops.append(top * scale)
        for c in range(tall):
            row_gram = spread(gram[p], c) * scales[c]
            row_unit = spread(unit[p], c) * scales[c]
            gram[p] = jnp.where(sub == c, row_gram, gram[p] - tops[c] * row_gram)
            unit[p] = jnp.where(sub == c, row_unit, unit[p] - tops[c] * row_unit)
        if more:
            rows = jnp.concatenate([gram[p], unit[p]], axis=1)
            high = rows.astype(jnp.bfloat16).astype(jnp.float32)
            low = rows - high
            left = jnp.concatenate([high[:, :size], high[:, :size], low[:, :size]], axis=0)
            right = jnp.concatenate([high, low, high], axis=0)
            taken = lax.dot_general(
                left.astype(jnp.bfloat16),
                right.astype(jnp.bfloat16),
                (((0,), (0,)), ((), ())),
                preferred_element_type=jnp.float32,
            )
            for t in range(p + 1, tiles):
                gram[t] = gram[t] - taken[tall * t : tall * (t + 1), :size]
                unit[t] = unit[t] - taken[tall * t : tall * (t + 1), size:]
        corner = ahead
    upper = [jnp.where(lanes >= sub + tall * t, gram[t], 0.0) for t in range(tiles)]
    return jnp.concatenate(upper, axis=0), jnp.concatenate(unit, axis=0)


def dot(a, b, right=0):
    (a_high, a_low), (b_high, b_low) = split(a), split(b)

    def product(x, y):
        return lax.dot_general(
            x, y, (((1,), (right,)), ((), ())), preferred_element_type=jnp.float32
        )

    return product(a_high, b_high) + (product(a_high, b_low) + product(a_low, b_high))


def column_kernel(place, first, scale, info, own, other, *refs):
    *refs, upper_out, inverse_out, gram = refs
    size = gram.shape[0]
    half = size // 2
    at = place * size
    for core, source in ((info[0], own), (1 - info[0], other)):
        rows = pl.ds(pl.multiple_of(core * half, half), half)
        for j in range(place + 1):
            gram[rows, j * size : (j + 1) * size] = source[(first + j) * half : (first + j + 1) * half, :]
    corner = gram[:, at:]
    if place:
        known, upper_known = refs
        left = dot(gram[:, :at], known[...], 1)
        corner = corner - dot(left, left, 1)
        carried = dot(left, known[...])
    upper, inverse = factor(corner)
    if place:
        inverse_out[at:, :at] = -dot(inverse, carried)
        inverse_out[:at, :at] = known[...]
        inverse_out[:at, at:] = jnp.zeros((at, size), jnp.float32)
        upper_out[:at, :at] = upper_known[...] * scale
        upper_out[at:, :at] = jnp.zeros((size, at), jnp.float32)
        upper_out[:at, at:] = left.T * scale
    inverse_out[at:, at:] = inverse
    upper_out[at:, at:] = upper * scale


def column(place, first, info, own, other, before, scale=1.0):
    whole = pl.BlockSpec(memory_space=pltpu.VMEM)
    size = own.shape[1]
    args = [own, other, *before]
    square = jax.ShapeDtypeStruct(((place + 1) * size,) * 2, jnp.float32)
    return pl.pallas_call(
        functools.partial(column_kernel, place, first, scale),
        in_specs=[pl.BlockSpec(memory_space=pltpu.SMEM)] + [whole] * len(args),
        out_specs=[whole, whole],
        out_shape=[square, square],
        scratch_shapes=[pltpu.VMEM((size, (place + 1) * size), jnp.float32)],
        compiler_params=pltpu.CompilerParams(vmem_limit_bytes=VMEM_LIMIT),
        cost_estimate=estimate(4.0),
        name="column",
    )(info, *args)


def basis_kernel(scale, count, *refs):
    *powers, inverse, out, high, low = refs
    columns = powers[0].shape[-1]

    @pl.when(pl.program_id(0) == 0)
    def _():
        high[...], low[...] = split(inverse[...] * scale)

    pairs = [split(p[...].reshape(-1, columns)) for p in powers]
    wide = 2 * columns
    for start in range(0, count * columns, wide):
        stop = min(start + wide, count * columns)
        left_high = jnp.concatenate([p[0] for p in pairs[: stop // columns]], axis=1)
        left_low = jnp.concatenate([p[1] for p in pairs[: stop // columns]], axis=1)
        acc = None
        for left, right in ((left_high, high), (left_low, high), (left_high, low)):
            term = lax.dot_general(
                left,
                right[start:stop, :stop],
                (((1,), (1,)), ((), ())),
                preferred_element_type=jnp.float32,
            )
            acc = term if acc is None else acc + term
        out[:, :, :, start:stop] = acc.astype(jnp.bfloat16).reshape(out.shape[:3] + (stop - start,))


def basis_of(powers, inverse, scale):
    layers, cross_local, size, columns = powers[0].shape
    count = len(powers)
    full = count * columns
    return pl.pallas_call(
        functools.partial(basis_kernel, scale, count),
        grid=(layers,),
        in_specs=[pl.BlockSpec((1, cross_local, size, columns), lambda i: (i, 0, 0, 0))] * count
        + [pl.BlockSpec(inverse.shape, lambda i: (0, 0))],
        out_specs=pl.BlockSpec((1, cross_local, size, full), lambda i: (i, 0, 0, 0)),
        out_shape=jax.ShapeDtypeStruct((layers, cross_local, size, full), jnp.bfloat16),
        scratch_shapes=[pltpu.VMEM((full, full), jnp.bfloat16)] * 2,
        compiler_params=pltpu.CompilerParams(vmem_limit_bytes=VMEM_LIMIT),
        cost_estimate=estimate(3.0),
        name="basis",
    )(*powers, inverse)


def local(sources, couplings, block_cols, lead_sites, lead_sigma):
    layers, cross_local, size, columns = sources.shape
    cross_count = lax.axis_size("cross")
    count = lax.axis_size("trans")
    place = lax.axis_index("trans")
    even = 1 - place % 2
    info = jnp.stack([lax.axis_index("cross"), place == 0, place == count - 1, even])
    info = info.astype(jnp.int32)
    packed = pack(couplings, lead_sites, lead_sigma, info)
    scale_rows = math.sqrt(count * layers * cross_local * cross_count * size)

    near = [(i, i ^ 1) for i in range(count) if i ^ 1 < count]
    far = [(i, j) for i in range(count) for j in (i - 1 + 2 * (i % 2),) if 0 <= j < count]

    def swap(x):
        return lax.ppermute(x, "cross", [(0, 1), (1, 0)])

    def exchange(x):
        return lax.all_to_all(x, "trans", 0, 0, tiled=True)

    def double(x, reach, work=None):
        other = lax.ppermute(x, "trans", [(i, i ^ reach) for i in range(count)])
        return x + (other if work is None else lax.optimization_barrier((other, work))[0])

    early = tuple((i, j) for i in range(S) for j in range(i + 1))
    powers = [sources]
    near_layer = lax.dynamic_slice_in_dim(sources, even * (layers - 1), 1)
    far_layer = lax.dynamic_slice_in_dim(sources, (1 - even) * (layers - 1), 1)
    for k in range(S):
        field = powers[k]
        near_edge = lax.ppermute(near_layer, "trans", near)
        far_edge = lax.ppermute(far_layer, "trans", far)
        other = swap(field)
        if k == 0:
            near_edge, far_edge, packed = lax.optimization_barrier((near_edge, far_edge, packed))
        if k == S - 1:
            mine, theirs = gram_blocks(powers, early, info, count)
            theirs, _, _ = lax.optimization_barrier((swap(theirs), near_edge, far_edge))
            parts = exchange((mine + theirs).reshape(count, -1, columns))
        edges = (near_edge, swap(near_edge), far_edge, swap(far_edge))
        before = powers[k - 1] if k else None
        got = step(packed, block_cols, info, field, other, edges, before, k == S - 1)
        powers.append(got[0])
        if k < S - 1:
            near_layer, far_layer = got[1:]
    mine, theirs = gram_blocks(powers, tuple((S, j) for j in range(S + 1)), info, count)
    last = mine + swap(theirs)
    last, parts = lax.optimization_barrier((last, parts))
    summed = jnp.sum(parts, axis=0, keepdims=True)
    known = exchange(jnp.broadcast_to(summed, parts.shape)).reshape(-1, columns)
    known_other = swap(known)
    first = column(0, 0, info, known, known_other, ())
    second = column(1, 1, info, known, known_other, first[::-1])
    third = column(2, 3, info, known, known_other, second[::-1])
    reach = 1
    while reach < count:
        work = third if 2 * reach == count else first if 4 * reach == count else None
        last = double(last, reach, work)
        reach *= 2
    r_factor, inverse = column(3, 0, info, last, swap(last), third[::-1], 1.0 / scale_rows)
    return basis_of(powers, inverse, scale_rows), r_factor


def solution(mesh):
    return jax.shard_map(
        local,
        mesh=mesh,
        in_specs=(
            P(("energy", "trans"), "cross", None, None),
            P(("energy", "trans"), "cross", None, None, None),
            P("trans", "cross", None),
            P(),
            P("energy", None, None),
        ),
        out_specs=(P(("energy", "trans"), "cross", None, None), P("energy", None)),
        check_vma=False,
    )
```

```python
import functools
import math

import jax
import jax.numpy as jnp
from jax import lax
from jax.experimental import pallas as pl
from jax.experimental.pallas import tpu as pltpu
from jax.sharding import PartitionSpec as P

S = 3
center_shift = 2.0
half_range = 1.6
VMEM_LIMIT = 16 * 1024 * 1024


def estimate(us):
    return pl.CostEstimate(flops=int(us * 1.15e9), bytes_accessed=0, transcendentals=0)


def split(x):
    high = x.astype(jnp.bfloat16)
    low = (x - high.astype(jnp.float32)).astype(jnp.bfloat16)
    return high, low


def pack_kernel(info, sites, held, leads, out):
    layers, cross_local, slots, size, _ = held.shape
    contacts = leads.shape[0]
    for layer in range(layers):
        for q in range(cross_local):
            place = info[0] * cross_local + q
            lead = jnp.zeros((size, size), jnp.float32)
            for k in range(contacts):
                end, flag = (0, info[1]) if k < contacts // 2 else (layers - 1, info[2])
                if layer == end:
                    here = jnp.logical_and(flag == 1, sites[k] == place)
                    lead = lead - leads[k] * jnp.where(here, 1.0, 0.0)
            blocks = [held[layer, q, j] for j in range(slots)] + [lead]
            row = jnp.concatenate(
                [jnp.concatenate(blocks[i : i + 2], axis=1) for i in range(0, slots + 1, 2)],
                axis=1,
            )
            high, low = split(row)
            out[layer * cross_local + q, :size] = high
            out[layer * cross_local + q, size:] = low


def pack(couplings, lead_sites, lead_sigma, info):
    layers, cross_local, slots, size, _ = couplings.shape
    scalar = pl.BlockSpec(memory_space=pltpu.SMEM)
    whole = pl.BlockSpec(memory_space=pltpu.VMEM)
    return pl.pallas_call(
        pack_kernel,
        in_specs=[scalar, scalar, whole, whole],
        out_specs=whole,
        out_shape=jax.ShapeDtypeStruct(
            (layers * cross_local, 2 * size, (slots + 1) * size), jnp.bfloat16
        ),
        compiler_params=pltpu.CompilerParams(vmem_limit_bytes=VMEM_LIMIT),
        cost_estimate=estimate(2.5),
        name="pack",
    )(info, lead_sites, couplings, lead_sigma)


def step_kernel(first, last, slots, info, cols, packed, own, other, *refs):
    edges, refs = refs[:4], refs[4:]
    before, refs = (None, refs) if first else (refs[0], refs[1:])
    out, field = refs[0], refs[-1]
    layers, cross_local, size, columns = own.shape
    total = 2 * cross_local
    mine = info[0] * cross_local
    theirs = (1 - info[0]) * cross_local

    def put(place, x):
        high, low = split(x)
        field[place, :, :columns] = high
        field[place, :, columns:] = low

    for layer in range(layers):
        for q in range(cross_local):
            put((layer + 1) * total + mine + q, own[layer, q])
            put((layer + 1) * total + theirs + q, other[layer, q])
    even = info[3]
    for pair, place in enumerate((even, 1 - even)):
        for q in range(cross_local):
            put(place * (layers + 1) * total + mine + q, edges[2 * pair][0, q])
            put(place * (layers + 1) * total + theirs + q, edges[2 * pair + 1][0, q])
    for layer in range(layers):
        for q in range(cross_local):
            row = layer * cross_local + q
            places = [cols[layer, q, j] for j in range(slots)] + [total + mine + q]
            picked = jnp.concatenate([field[layer * total + c] for c in places], axis=0)
            acc = jnp.dot(packed[row], picked, preferred_element_type=jnp.float32)
            acc = acc[:, :columns] + acc[:, columns:]
            applied = acc[:size] + acc[size:]
            value = (applied - center_shift * own[layer, q]) * (1.0 / half_range)
            if not first:
                value = 2.0 * value - before[layer, q]
            out[layer, q] = value
    if not last:
        refs[1][0] = out[even * (layers - 1)]
        refs[2][0] = out[(1 - even) * (layers - 1)]


def step(packed, cols, info, own, other, edges, before, last):
    layers, cross_local, size, columns = own.shape
    rows, _, depth = packed.shape
    whole = pl.BlockSpec(memory_space=pltpu.VMEM)
    scalar = pl.BlockSpec(memory_space=pltpu.SMEM)
    args = [packed, own, other, *edges] + ([] if before is None else [before])
    edge = jax.ShapeDtypeStruct((1,) + own.shape[1:], jnp.float32)
    shapes = [jax.ShapeDtypeStruct(own.shape, jnp.float32)] + ([] if last else [edge, edge])
    return pl.pallas_call(
        functools.partial(step_kernel, before is None, last, cols.shape[2]),
        in_specs=[scalar, scalar] + [whole] * len(args),
        out_specs=[whole] * len(shapes),
        out_shape=shapes,
        scratch_shapes=[
            pltpu.VMEM(((layers + 2) * 2 * cross_local, size, 2 * columns), jnp.bfloat16)
        ],
        cost_estimate=estimate(1.7),
        compiler_params=pltpu.CompilerParams(vmem_limit_bytes=VMEM_LIMIT),
        name="step",
    )(info, cols, *args)


def gram_kernel(pairs, info, *refs):
    *powers, mine, theirs, block, held = refs
    columns = mine.shape[1]
    half = columns // 2
    for j, power in enumerate(powers):
        high, low = split(power[...].reshape(-1, columns))
        held[j, :, :columns] = high
        held[j, :, columns:] = low
    for place, (i, j) in enumerate(pairs):
        acc = lax.dot_general(
            held[i], held[j], (((0,), (0,)), ((), ())), preferred_element_type=jnp.float32
        )
        acc = acc[:, :columns] + acc[:, columns:]
        block[place] = acc[:columns] + acc[columns:]
        for core, out in ((info[0], mine), (1 - info[0], theirs)):
            rows = pl.ds(pl.multiple_of(core * half, half), half)
            out[place * half : (place + 1) * half, :] = block[place, rows, :]
    used = len(pairs) * half
    if used < mine.shape[0]:
        for out in (mine, theirs):
            out[used:, :] = jnp.zeros((mine.shape[0] - used, columns), jnp.float32)


def gram_blocks(powers, pairs, info, count):
    columns = powers[0].shape[-1]
    rows = powers[0].size // columns
    whole = pl.BlockSpec(memory_space=pltpu.VMEM)
    tall = share(len(pairs), columns, count) * count
    return pl.pallas_call(
        functools.partial(gram_kernel, pairs),
        in_specs=[pl.BlockSpec(memory_space=pltpu.SMEM)] + [whole] * len(powers),
        out_specs=[whole] * 2,
        out_shape=[jax.ShapeDtypeStruct((tall, columns), jnp.float32)] * 2,
        scratch_shapes=[
            pltpu.VMEM((len(pairs), columns, columns), jnp.float32),
            pltpu.VMEM((len(powers), rows, 2 * columns), jnp.bfloat16),
        ],
        cost_estimate=estimate(1.4),
        compiler_params=pltpu.CompilerParams(vmem_limit_bytes=VMEM_LIMIT),
        name="gram",
    )(info, *powers)


def share(blocks, columns, count):
    return -(-blocks * (columns // 2) // count)


def factor(block):
    size = block.shape[0]
    tall = 8
    tiles = size // tall
    lanes = lax.broadcasted_iota(jnp.int32, (tall, size), 1)
    sub = lax.broadcasted_iota(jnp.int32, (tall, size), 0)
    gram = [block[tall * t : tall * (t + 1)] for t in range(tiles)]
    unit = [jnp.where(lanes == sub + tall * t, 1.0, 0.0) for t in range(tiles)]

    def spread(x, row):
        return jnp.broadcast_to(x[row : row + 1], (tall, size))

    def lane(x, at):
        return jnp.broadcast_to(x[:, at : at + 1], (tall, size))

    corner = [lane(gram[0], c) for c in range(tall)]
    for p in range(tiles):
        at = tall * p
        below = range(p + 1, tiles)
        cols = [[lane(gram[t], at + c) for t in below] for c in range(tall)]
        ahead = [lane(gram[p + 1], at + tall + d) for d in range(tall)] if p + 1 < tiles else []
        scales, tops, lows = [], [], []
        for c in range(tall):
            scale = lax.rsqrt(spread(corner[c], c))
            square = scale * scale
            top = jnp.where(sub > c, corner[c], 0.0)
            weights = [spread(corner[d], c) for d in range(c + 1, tall)]
            for d in range(c + 1, tall):
                corner[d] = corner[d] - (top * weights[d - c - 1]) * square
            low = [x * scale for x in cols[c]]
            for d in range(c + 1, tall):
                weight = weights[d - c - 1] * scale
                cols[d] = [x - m * weight for x, m in zip(cols[d], low)]
            if low:
                ahead = [x - low[0] * spread(low[0], d) for d, x in enumerate(ahead)]
            scales.append(scale)
            tops.append(top * scale)
            lows.append(low)
        for c in range(tall):
            row_gram = spread(gram[p], c) * scales[c]
            row_unit = spread(unit[p], c) * scales[c]
            gram[p] = jnp.where(sub == c, row_gram, gram[p] - tops[c] * row_gram)
            unit[p] = jnp.where(sub == c, row_unit, unit[p] - tops[c] * row_unit)
            for t, m in zip(below, lows[c]):
                gram[t] = gram[t] - m * row_gram
                unit[t] = unit[t] - m * row_unit
        corner = ahead
    upper = [jnp.where(lanes >= sub + tall * t, gram[t], 0.0) for t in range(tiles)]
    return jnp.concatenate(upper, axis=0), jnp.concatenate(unit, axis=0)


def dot(a, b, right=0):
    (a_high, a_low), (b_high, b_low) = split(a), split(b)

    def product(x, y):
        return lax.dot_general(
            x, y, (((1,), (right,)), ((), ())), preferred_element_type=jnp.float32
        )

    return product(a_high, b_high) + (product(a_high, b_low) + product(a_low, b_high))


def column_kernel(place, first, scale, info, own, other, *refs):
    *refs, upper_out, inverse_out, gram = refs
    size = gram.shape[0]
    half = size // 2
    at = place * size
    for core, source in ((info[0], own), (1 - info[0], other)):
        rows = pl.ds(pl.multiple_of(core * half, half), half)
        for j in range(place + 1):
            gram[rows, j * size : (j + 1) * size] = source[(first + j) * half : (first + j + 1) * half, :]
    corner = gram[:, at:]
    if place:
        known, upper_known = refs
        left = dot(gram[:, :at], known[...], 1)
        corner = corner - dot(left, left, 1)
        carried = dot(left, known[...])
    upper, inverse = factor(corner)
    if place:
        inverse_out[at:, :at] = -dot(inverse, carried)
        inverse_out[:at, :at] = known[...]
        inverse_out[:at, at:] = jnp.zeros((at, size), jnp.float32)
        upper_out[:at, :at] = upper_known[...] * scale
        upper_out[at:, :at] = jnp.zeros((size, at), jnp.float32)
        upper_out[:at, at:] = left.T * scale
    inverse_out[at:, at:] = inverse
    upper_out[at:, at:] = upper * scale


def column(place, first, info, own, other, before, scale=1.0):
    whole = pl.BlockSpec(memory_space=pltpu.VMEM)
    size = own.shape[1]
    args = [own, other, *before]
    square = jax.ShapeDtypeStruct(((place + 1) * size,) * 2, jnp.float32)
    return pl.pallas_call(
        functools.partial(column_kernel, place, first, scale),
        in_specs=[pl.BlockSpec(memory_space=pltpu.SMEM)] + [whole] * len(args),
        out_specs=[whole, whole],
        out_shape=[square, square],
        scratch_shapes=[pltpu.VMEM((size, (place + 1) * size), jnp.float32)],
        compiler_params=pltpu.CompilerParams(vmem_limit_bytes=VMEM_LIMIT),
        cost_estimate=estimate(4.0),
        name="column",
    )(info, *args)


def basis_kernel(scale, count, *refs):
    *powers, inverse, out, high, low = refs
    columns = powers[0].shape[-1]

    @pl.when(pl.program_id(0) == 0)
    def _():
        high[...], low[...] = split(inverse[...] * scale)

    pairs = [split(p[...].reshape(-1, columns)) for p in powers]
    wide = 2 * columns
    for start in range(0, count * columns, wide):
        stop = min(start + wide, count * columns)
        left_high = jnp.concatenate([p[0] for p in pairs[: stop // columns]], axis=1)
        left_low = jnp.concatenate([p[1] for p in pairs[: stop // columns]], axis=1)
        acc = None
        for left, right in ((left_high, high), (left_low, high), (left_high, low)):
            term = lax.dot_general(
                left,
                right[start:stop, :stop],
                (((1,), (1,)), ((), ())),
                preferred_element_type=jnp.float32,
            )
            acc = term if acc is None else acc + term
        out[:, :, :, start:stop] = acc.astype(jnp.bfloat16).reshape(out.shape[:3] + (stop - start,))


def basis_of(powers, inverse, scale):
    layers, cross_local, size, columns = powers[0].shape
    count = len(powers)
    full = count * columns
    return pl.pallas_call(
        functools.partial(basis_kernel, scale, count),
        grid=(layers,),
        in_specs=[pl.BlockSpec((1, cross_local, size, columns), lambda i: (i, 0, 0, 0))] * count
        + [pl.BlockSpec(inverse.shape, lambda i: (0, 0))],
        out_specs=pl.BlockSpec((1, cross_local, size, full), lambda i: (i, 0, 0, 0)),
        out_shape=jax.ShapeDtypeStruct((layers, cross_local, size, full), jnp.bfloat16),
        scratch_shapes=[pltpu.VMEM((full, full), jnp.bfloat16)] * 2,
        compiler_params=pltpu.CompilerParams(vmem_limit_bytes=VMEM_LIMIT),
        cost_estimate=estimate(3.0),
        name="basis",
    )(*powers, inverse)


def local(sources, couplings, block_cols, lead_sites, lead_sigma):
    layers, cross_local, size, columns = sources.shape
    cross_count = lax.axis_size("cross")
    count = lax.axis_size("trans")
    place = lax.axis_index("trans")
    even = 1 - place % 2
    info = jnp.stack([lax.axis_index("cross"), place == 0, place == count - 1, even])
    info = info.astype(jnp.int32)
    packed = pack(couplings, lead_sites, lead_sigma, info)
    scale_rows = math.sqrt(count * layers * cross_local * cross_count * size)

    near = [(i, i ^ 1) for i in range(count) if i ^ 1 < count]
    far = [(i, j) for i in range(count) for j in (i - 1 + 2 * (i % 2),) if 0 <= j < count]

    def swap(x):
        return lax.ppermute(x, "cross", [(0, 1), (1, 0)])

    def exchange(x):
        return lax.all_to_all(x, "trans", 0, 0, tiled=True)

    def double(x, reach, work=None):
        other = lax.ppermute(x, "trans", [(i, i ^ reach) for i in range(count)])
        return x + (other if work is None else lax.optimization_barrier((other, work))[0])

    early = tuple((i, j) for i in range(S) for j in range(i + 1))
    powers = [sources]
    near_layer = lax.dynamic_slice_in_dim(sources, even * (layers - 1), 1)
    far_layer = lax.dynamic_slice_in_dim(sources, (1 - even) * (layers - 1), 1)
    for k in range(S):
        field = powers[k]
        near_edge = lax.ppermute(near_layer, "trans", near)
        far_edge = lax.ppermute(far_layer, "trans", far)
        other = swap(field)
        if k == 0:
            far_edge, near_edge, packed = lax.optimization_barrier((far_edge, near_edge, packed))
        if k == S - 1:
            mine, theirs = gram_blocks(powers, early, info, count)
            theirs, _, _ = lax.optimization_barrier((swap(theirs), near_edge, far_edge))
            parts = exchange((mine + theirs).reshape(count, -1, columns))
        edges = (near_edge, swap(near_edge), far_edge, swap(far_edge))
        before = powers[k - 1] if k else None
        got = step(packed, block_cols, info, field, other, edges, before, k == S - 1)
        powers.append(got[0])
        if k < S - 1:
            near_layer, far_layer = got[1:]
    mine, theirs = gram_blocks(powers, tuple((S, j) for j in range(S + 1)), info, count)
    last = mine + swap(theirs)
    last, parts = lax.optimization_barrier((last, parts))
    summed = jnp.sum(parts, axis=0, keepdims=True)
    known = exchange(jnp.broadcast_to(summed, parts.shape))
    last = double(last, 1)
    known, _ = lax.optimization_barrier((known, last))
    known = known.reshape(-1, columns)
    known_other = swap(known)
    first = column(0, 0, info, known, known_other, ())
    second = column(1, 1, info, known, known_other, first[::-1])
    third = column(2, 3, info, known, known_other, second[::-1])
    reach = 2
    while reach < count:
        work = third if 2 * reach == count else first if 4 * reach == count else None
        last = double(last, reach, work)
        reach *= 2
    r_factor, inverse = column(3, 0, info, last, swap(last), third[::-1], 1.0 / scale_rows)
    return basis_of(powers, inverse, scale_rows), r_factor


def solution(mesh):
    return jax.shard_map(
        local,
        mesh=mesh,
        in_specs=(
            P(("energy", "trans"), "cross", None, None),
            P(("energy", "trans"), "cross", None, None, None),
            P("trans", "cross", None),
            P(),
            P("energy", None, None),
        ),
        out_specs=(P(("energy", "trans"), "cross", None, None), P("energy", None)),
        check_vma=False,
    )
```

```python
import functools
import math

import jax
import jax.numpy as jnp
from jax import lax
from jax.experimental import pallas as pl
from jax.experimental.pallas import tpu as pltpu
from jax.sharding import PartitionSpec as P

S = 3
center_shift = 2.0
half_range = 1.6
VMEM_LIMIT = 16 * 1024 * 1024


def estimate(us):
    return pl.CostEstimate(flops=int(us * 1.15e9), bytes_accessed=0, transcendentals=0)


def split(x):
    high = x.astype(jnp.bfloat16)
    low = (x - high.astype(jnp.float32)).astype(jnp.bfloat16)
    return high, low


def pack_kernel(info, sites, held, leads, out):
    layers, cross_local, slots, size, _ = held.shape
    contacts = leads.shape[0]
    for layer in range(layers):
        for q in range(cross_local):
            place = info[0] * cross_local + q
            lead = jnp.zeros((size, size), jnp.float32)
            for k in range(contacts):
                end, flag = (0, info[1]) if k < contacts // 2 else (layers - 1, info[2])
                if layer == end:
                    here = jnp.logical_and(flag == 1, sites[k] == place)
                    lead = lead - leads[k] * jnp.where(here, 1.0, 0.0)
            blocks = [held[layer, q, j] for j in range(slots)] + [lead]
            row = jnp.concatenate(
                [jnp.concatenate(blocks[i : i + 2], axis=1) for i in range(0, slots + 1, 2)],
                axis=1,
            )
            high, low = split(row)
            out[layer * cross_local + q, :size] = high
            out[layer * cross_local + q, size:] = low


def pack(couplings, lead_sites, lead_sigma, info):
    layers, cross_local, slots, size, _ = couplings.shape
    scalar = pl.BlockSpec(memory_space=pltpu.SMEM)
    whole = pl.BlockSpec(memory_space=pltpu.VMEM)
    return pl.pallas_call(
        pack_kernel,
        in_specs=[scalar, scalar, whole, whole],
        out_specs=whole,
        out_shape=jax.ShapeDtypeStruct(
            (layers * cross_local, 2 * size, (slots + 1) * size), jnp.bfloat16
        ),
        compiler_params=pltpu.CompilerParams(vmem_limit_bytes=VMEM_LIMIT),
        cost_estimate=estimate(2.5),
        name="pack",
    )(info, lead_sites, couplings, lead_sigma)


def step_kernel(first, last, slots, info, cols, packed, own, other, *refs):
    edges, refs = refs[:4], refs[4:]
    before, refs = (None, refs) if first else (refs[0], refs[1:])
    out, field = refs[0], refs[-1]
    layers, cross_local, size, columns = own.shape
    total = 2 * cross_local
    mine = info[0] * cross_local
    theirs = (1 - info[0]) * cross_local

    def put(place, x):
        high, low = split(x)
        field[place, :, :columns] = high
        field[place, :, columns:] = low

    for layer in range(layers):
        for q in range(cross_local):
            put((layer + 1) * total + mine + q, own[layer, q])
            put((layer + 1) * total + theirs + q, other[layer, q])
    even = info[3]
    for pair, place in enumerate((even, 1 - even)):
        for q in range(cross_local):
            put(place * (layers + 1) * total + mine + q, edges[2 * pair][0, q])
            put(place * (layers + 1) * total + theirs + q, edges[2 * pair + 1][0, q])
    for layer in range(layers):
        for q in range(cross_local):
            row = layer * cross_local + q
            places = [cols[layer, q, j] for j in range(slots)] + [total + mine + q]
            picked = jnp.concatenate([field[layer * total + c] for c in places], axis=0)
            acc = jnp.dot(packed[row], picked, preferred_element_type=jnp.float32)
            acc = acc[:, :columns] + acc[:, columns:]
            applied = acc[:size] + acc[size:]
            value = (applied - center_shift * own[layer, q]) * (1.0 / half_range)
            if not first:
                value = 2.0 * value - before[layer, q]
            out[layer, q] = value
    if not last:
        refs[1][0] = out[even * (layers - 1)]
        refs[2][0] = out[(1 - even) * (layers - 1)]


def step(packed, cols, info, own, other, edges, before, last):
    layers, cross_local, size, columns = own.shape
    rows, _, depth = packed.shape
    whole = pl.BlockSpec(memory_space=pltpu.VMEM)
    scalar = pl.BlockSpec(memory_space=pltpu.SMEM)
    args = [packed, own, other, *edges] + ([] if before is None else [before])
    edge = jax.ShapeDtypeStruct((1,) + own.shape[1:], jnp.float32)
    shapes = [jax.ShapeDtypeStruct(own.shape, jnp.float32)] + ([] if last else [edge, edge])
    return pl.pallas_call(
        functools.partial(step_kernel, before is None, last, cols.shape[2]),
        in_specs=[scalar, scalar] + [whole] * len(args),
        out_specs=[whole] * len(shapes),
        out_shape=shapes,
        scratch_shapes=[
            pltpu.VMEM(((layers + 2) * 2 * cross_local, size, 2 * columns), jnp.bfloat16)
        ],
        cost_estimate=estimate(1.7),
        compiler_params=pltpu.CompilerParams(vmem_limit_bytes=VMEM_LIMIT),
        name="step",
    )(info, cols, *args)


def gram_kernel(pairs, info, *refs):
    *powers, mine, theirs, block, held = refs
    columns = mine.shape[1]
    half = columns // 2
    for j, power in enumerate(powers):
        high, low = split(power[...].reshape(-1, columns))
        held[j, :, :columns] = high
        held[j, :, columns:] = low
    for place, (i, j) in enumerate(pairs):
        acc = lax.dot_general(
            held[i], held[j], (((0,), (0,)), ((), ())), preferred_element_type=jnp.float32
        )
        acc = acc[:, :columns] + acc[:, columns:]
        block[place] = acc[:columns] + acc[columns:]
        for core, out in ((info[0], mine), (1 - info[0], theirs)):
            rows = pl.ds(pl.multiple_of(core * half, half), half)
            out[place * half : (place + 1) * half, :] = block[place, rows, :]
    used = len(pairs) * half
    if used < mine.shape[0]:
        for out in (mine, theirs):
            out[used:, :] = jnp.zeros((mine.shape[0] - used, columns), jnp.float32)


def gram_blocks(powers, pairs, info, count):
    columns = powers[0].shape[-1]
    rows = powers[0].size // columns
    whole = pl.BlockSpec(memory_space=pltpu.VMEM)
    tall = share(len(pairs), columns, count) * count
    return pl.pallas_call(
        functools.partial(gram_kernel, pairs),
        in_specs=[pl.BlockSpec(memory_space=pltpu.SMEM)] + [whole] * len(powers),
        out_specs=[whole] * 2,
        out_shape=[jax.ShapeDtypeStruct((tall, columns), jnp.float32)] * 2,
        scratch_shapes=[
            pltpu.VMEM((len(pairs), columns, columns), jnp.float32),
            pltpu.VMEM((len(powers), rows, 2 * columns), jnp.bfloat16),
        ],
        cost_estimate=estimate(1.4),
        compiler_params=pltpu.CompilerParams(vmem_limit_bytes=VMEM_LIMIT),
        name="gram",
    )(info, *powers)


def share(blocks, columns, count):
    return -(-blocks * (columns // 2) // count)


def factor(block):
    size = block.shape[0]
    tall = 8
    tiles = size // tall
    lanes = lax.broadcasted_iota(jnp.int32, (tall, size), 1)
    sub = lax.broadcasted_iota(jnp.int32, (tall, size), 0)
    gram = [block[tall * t : tall * (t + 1)] for t in range(tiles)]
    unit = [jnp.where(lanes == sub + tall * t, 1.0, 0.0) for t in range(tiles)]

    def spread(x, row):
        return jnp.broadcast_to(x[row : row + 1], (tall, size))

    def lane(x, at):
        return jnp.broadcast_to(x[:, at : at + 1], (tall, size))

    corner = [lane(gram[0], c) for c in range(tall)]
    for p in range(tiles):
        at = tall * p
        below = range(p + 1, tiles)
        cols = [[lane(gram[t], at + c) for t in below] for c in range(tall)]
        ahead = [lane(gram[p + 1], at + tall + d) for d in range(tall)] if p + 1 < tiles else []
        entry = {(d, c): spread(corner[c], d) for c in range(tall) for d in range(c, tall)}
        scales, tops, lows = [], [], []
        for c in range(tall):
            scale = lax.rsqrt(entry[c, c])
            weights = [entry[d, c] * scale for d in range(c + 1, tall)]
            for e in range(c + 1, tall):
                for d in range(e, tall):
                    entry[d, e] = entry[d, e] - weights[d - c - 1] * weights[e - c - 1]
            top = jnp.where(sub > c, corner[c], 0.0) * scale
            for d in range(c + 1, tall):
                corner[d] = corner[d] - top * weights[d - c - 1]
            low = [x * scale for x in cols[c]]
            for d in range(c + 1, tall):
                cols[d] = [x - m * weights[d - c - 1] for x, m in zip(cols[d], low)]
            if low:
                ahead = [x - low[0] * spread(low[0], d) for d, x in enumerate(ahead)]
            scales.append(scale)
            tops.append(top)
            lows.append(low)
        for c in range(tall):
            row_gram = spread(gram[p], c) * scales[c]
            row_unit = spread(unit[p], c) * scales[c]
            gram[p] = jnp.where(sub == c, row_gram, gram[p] - tops[c] * row_gram)
            unit[p] = jnp.where(sub == c, row_unit, unit[p] - tops[c] * row_unit)
            for t, m in zip(below, lows[c]):
                gram[t] = gram[t] - m * row_gram
                unit[t] = unit[t] - m * row_unit
        corner = ahead
    upper = [jnp.where(lanes >= sub + tall * t, gram[t], 0.0) for t in range(tiles)]
    return jnp.concatenate(upper, axis=0), jnp.concatenate(unit, axis=0)


def dot(a, b, right=0):
    (a_high, a_low), (b_high, b_low) = split(a), split(b)

    def product(x, y):
        return lax.dot_general(
            x, y, (((1,), (right,)), ((), ())), preferred_element_type=jnp.float32
        )

    return product(a_high, b_high) + (product(a_high, b_low) + product(a_low, b_high))


def column_kernel(place, first, scale, info, own, other, *refs):
    *refs, upper_out, inverse_out, gram = refs
    size = gram.shape[0]
    half = size // 2
    at = place * size
    for core, source in ((info[0], own), (1 - info[0], other)):
        rows = pl.ds(pl.multiple_of(core * half, half), half)
        for j in range(place + 1):
            gram[rows, j * size : (j + 1) * size] = source[(first + j) * half : (first + j + 1) * half, :]
    corner = gram[:, at:]
    if place:
        known, upper_known = refs
        left = dot(gram[:, :at], known[...], 1)
        corner = corner - dot(left, left, 1)
        carried = dot(left, known[...])
    upper, inverse = factor(corner)
    if place:
        inverse_out[at:, :at] = -dot(inverse, carried)
        inverse_out[:at, :at] = known[...]
        inverse_out[:at, at:] = jnp.zeros((at, size), jnp.float32)
        upper_out[:at, :at] = upper_known[...] * scale
        upper_out[at:, :at] = jnp.zeros((size, at), jnp.float32)
        upper_out[:at, at:] = left.T * scale
    inverse_out[at:, at:] = inverse
    upper_out[at:, at:] = upper * scale


def column(place, first, info, own, other, before, scale=1.0):
    whole = pl.BlockSpec(memory_space=pltpu.VMEM)
    size = own.shape[1]
    args = [own, other, *before]
    square = jax.ShapeDtypeStruct(((place + 1) * size,) * 2, jnp.float32)
    return pl.pallas_call(
        functools.partial(column_kernel, place, first, scale),
        in_specs=[pl.BlockSpec(memory_space=pltpu.SMEM)] + [whole] * len(args),
        out_specs=[whole, whole],
        out_shape=[square, square],
        scratch_shapes=[pltpu.VMEM((size, (place + 1) * size), jnp.float32)],
        compiler_params=pltpu.CompilerParams(vmem_limit_bytes=VMEM_LIMIT),
        cost_estimate=estimate(4.0),
        name="column",
    )(info, *args)


def basis_kernel(scale, count, *refs):
    *powers, inverse, out, high, low = refs
    columns = powers[0].shape[-1]

    @pl.when(pl.program_id(0) == 0)
    def _():
        high[...], low[...] = split(inverse[...] * scale)

    pairs = [split(p[...].reshape(-1, columns)) for p in powers]
    wide = 2 * columns
    for start in range(0, count * columns, wide):
        stop = min(start + wide, count * columns)
        left_high = jnp.concatenate([p[0] for p in pairs[: stop // columns]], axis=1)
        left_low = jnp.concatenate([p[1] for p in pairs[: stop // columns]], axis=1)
        acc = None
        for left, right in ((left_high, high), (left_low, high), (left_high, low)):
            term = lax.dot_general(
                left,
                right[start:stop, :stop],
                (((1,), (1,)), ((), ())),
                preferred_element_type=jnp.float32,
            )
            acc = term if acc is None else acc + term
        out[:, :, :, start:stop] = acc.astype(jnp.bfloat16).reshape(out.shape[:3] + (stop - start,))


def basis_of(powers, inverse, scale):
    layers, cross_local, size, columns = powers[0].shape
    count = len(powers)
    full = count * columns
    return pl.pallas_call(
        functools.partial(basis_kernel, scale, count),
        grid=(layers,),
        in_specs=[pl.BlockSpec((1, cross_local, size, columns), lambda i: (i, 0, 0, 0))] * count
        + [pl.BlockSpec(inverse.shape, lambda i: (0, 0))],
        out_specs=pl.BlockSpec((1, cross_local, size, full), lambda i: (i, 0, 0, 0)),
        out_shape=jax.ShapeDtypeStruct((layers, cross_local, size, full), jnp.bfloat16),
        scratch_shapes=[pltpu.VMEM((full, full), jnp.bfloat16)] * 2,
        compiler_params=pltpu.CompilerParams(vmem_limit_bytes=VMEM_LIMIT),
        cost_estimate=estimate(3.0),
        name="basis",
    )(*powers, inverse)


def local(sources, couplings, block_cols, lead_sites, lead_sigma):
    layers, cross_local, size, columns = sources.shape
    cross_count = lax.axis_size("cross")
    count = lax.axis_size("trans")
    place = lax.axis_index("trans")
    even = 1 - place % 2
    info = jnp.stack([lax.axis_index("cross"), place == 0, place == count - 1, even])
    info = info.astype(jnp.int32)
    packed = pack(couplings, lead_sites, lead_sigma, info)
    scale_rows = math.sqrt(count * layers * cross_local * cross_count * size)

    near = [(i, i ^ 1) for i in range(count) if i ^ 1 < count]
    far = [(i, j) for i in range(count) for j in (i - 1 + 2 * (i % 2),) if 0 <= j < count]

    def swap(x):
        return lax.ppermute(x, "cross", [(0, 1), (1, 0)])

    def exchange(x):
        return lax.all_to_all(x, "trans", 0, 0, tiled=True)

    def double(x, reach, work=None):
        other = lax.ppermute(x, "trans", [(i, i ^ reach) for i in range(count)])
        return x + (other if work is None else lax.optimization_barrier((other, work))[0])

    early = tuple((i, j) for i in range(S) for j in range(i + 1))
    powers = [sources]
    near_layer = lax.dynamic_slice_in_dim(sources, even * (layers - 1), 1)
    far_layer = lax.dynamic_slice_in_dim(sources, (1 - even) * (layers - 1), 1)
    for k in range(S):
        field = powers[k]
        near_edge = lax.ppermute(near_layer, "trans", near)
        far_edge = lax.ppermute(far_layer, "trans", far)
        other = swap(field)
        if k == 0:
            far_edge, near_edge, packed = lax.optimization_barrier((far_edge, near_edge, packed))
        if k == S - 1:
            mine, theirs = gram_blocks(powers, early, info, count)
            theirs, _, _ = lax.optimization_barrier((swap(theirs), near_edge, far_edge))
            parts = exchange((mine + theirs).reshape(count, -1, columns))
        edges = (near_edge, swap(near_edge), far_edge, swap(far_edge))
        before = powers[k - 1] if k else None
        got = step(packed, block_cols, info, field, other, edges, before, k == S - 1)
        powers.append(got[0])
        if k < S - 1:
            near_layer, far_layer = got[1:]
    mine, theirs = gram_blocks(powers, tuple((S, j) for j in range(S + 1)), info, count)
    last = mine + swap(theirs)
    last, parts = lax.optimization_barrier((last, parts))
    summed = jnp.sum(parts, axis=0, keepdims=True)
    known = exchange(jnp.broadcast_to(summed, parts.shape))
    last = double(last, 1)
    known, _ = lax.optimization_barrier((known, last))
    known = known.reshape(-1, columns)
    known_other = swap(known)
    first = column(0, 0, info, known, known_other, ())
    second = column(1, 1, info, known, known_other, first[::-1])
    third = column(2, 3, info, known, known_other, second[::-1])
    reach = 2
    while reach < count:
        work = third if 2 * reach == count else first if 4 * reach == count else None
        last = double(last, reach, work)
        reach *= 2
    r_factor, inverse = column(3, 0, info, last, swap(last), third[::-1], 1.0 / scale_rows)
    return basis_of(powers, inverse, scale_rows), r_factor


def solution(mesh):
    return jax.shard_map(
        local,
        mesh=mesh,
        in_specs=(
            P(("energy", "trans"), "cross", None, None),
            P(("energy", "trans"), "cross", None, None, None),
            P("trans", "cross", None),
            P(),
            P("energy", None, None),
        ),
        out_specs=(P(("energy", "trans"), "cross", None, None), P("energy", None)),
        check_vma=False,
    )
```

```python
import functools
import math

import jax
import jax.numpy as jnp
from jax import lax
from jax.experimental import pallas as pl
from jax.experimental.pallas import tpu as pltpu
from jax.sharding import PartitionSpec as P

S = 3
center_shift = 2.0
half_range = 1.6
VMEM_LIMIT = 16 * 1024 * 1024


def estimate(us):
    return pl.CostEstimate(flops=int(us * 1.15e9), bytes_accessed=0, transcendentals=0)


def split(x):
    high = x.astype(jnp.bfloat16)
    low = (x - high.astype(jnp.float32)).astype(jnp.bfloat16)
    return high, low


def pack_kernel(info, sites, held, leads, out):
    layers, cross_local, slots, size, _ = held.shape
    contacts = leads.shape[0]
    for layer in range(layers):
        for q in range(cross_local):
            place = info[0] * cross_local + q
            lead = jnp.zeros((size, size), jnp.float32)
            for k in range(contacts):
                end, flag = (0, info[1]) if k < contacts // 2 else (layers - 1, info[2])
                if layer == end:
                    here = jnp.logical_and(flag == 1, sites[k] == place)
                    lead = lead - leads[k] * jnp.where(here, 1.0, 0.0)
            blocks = [held[layer, q, j] for j in range(slots)] + [lead]
            row = jnp.concatenate(
                [jnp.concatenate(blocks[i : i + 2], axis=1) for i in range(0, slots + 1, 2)],
                axis=1,
            )
            high, low = split(row)
            out[layer * cross_local + q, :size] = high
            out[layer * cross_local + q, size:] = low


def pack(couplings, lead_sites, lead_sigma, info):
    layers, cross_local, slots, size, _ = couplings.shape
    scalar = pl.BlockSpec(memory_space=pltpu.SMEM)
    whole = pl.BlockSpec(memory_space=pltpu.VMEM)
    return pl.pallas_call(
        pack_kernel,
        in_specs=[scalar, scalar, whole, whole],
        out_specs=whole,
        out_shape=jax.ShapeDtypeStruct(
            (layers * cross_local, 2 * size, (slots + 1) * size), jnp.bfloat16
        ),
        compiler_params=pltpu.CompilerParams(vmem_limit_bytes=VMEM_LIMIT),
        cost_estimate=estimate(2.5),
        name="pack",
    )(info, lead_sites, couplings, lead_sigma)


def step_kernel(first, last, slots, info, cols, packed, own, other, *refs):
    edges, refs = refs[:4], refs[4:]
    before, refs = (None, refs) if first else (refs[0], refs[1:])
    out, field = refs[0], refs[-1]
    layers, cross_local, size, columns = own.shape
    total = 2 * cross_local
    mine = info[0] * cross_local
    theirs = (1 - info[0]) * cross_local

    def put(place, x):
        high, low = split(x)
        field[place, :, :columns] = high
        field[place, :, columns:] = low

    for layer in range(layers):
        for q in range(cross_local):
            put((layer + 1) * total + mine + q, own[layer, q])
            put((layer + 1) * total + theirs + q, other[layer, q])
    even = info[3]
    for pair, place in enumerate((even, 1 - even)):
        for q in range(cross_local):
            put(place * (layers + 1) * total + mine + q, edges[2 * pair][0, q])
            put(place * (layers + 1) * total + theirs + q, edges[2 * pair + 1][0, q])
    for layer in range(layers):
        for q in range(cross_local):
            row = layer * cross_local + q
            places = [cols[layer, q, j] for j in range(slots)] + [total + mine + q]
            picked = jnp.concatenate([field[layer * total + c] for c in places], axis=0)
            acc = jnp.dot(packed[row], picked, preferred_element_type=jnp.float32)
            acc = acc[:, :columns] + acc[:, columns:]
            applied = acc[:size] + acc[size:]
            value = (applied - center_shift * own[layer, q]) * (1.0 / half_range)
            if not first:
                value = 2.0 * value - before[layer, q]
            out[layer, q] = value
    if not last:
        refs[1][0] = out[even * (layers - 1)]
        refs[2][0] = out[(1 - even) * (layers - 1)]


def step(packed, cols, info, own, other, edges, before, last):
    layers, cross_local, size, columns = own.shape
    rows, _, depth = packed.shape
    whole = pl.BlockSpec(memory_space=pltpu.VMEM)
    scalar = pl.BlockSpec(memory_space=pltpu.SMEM)
    args = [packed, own, other, *edges] + ([] if before is None else [before])
    edge = jax.ShapeDtypeStruct((1,) + own.shape[1:], jnp.float32)
    shapes = [jax.ShapeDtypeStruct(own.shape, jnp.float32)] + ([] if last else [edge, edge])
    return pl.pallas_call(
        functools.partial(step_kernel, before is None, last, cols.shape[2]),
        in_specs=[scalar, scalar] + [whole] * len(args),
        out_specs=[whole] * len(shapes),
        out_shape=shapes,
        scratch_shapes=[
            pltpu.VMEM(((layers + 2) * 2 * cross_local, size, 2 * columns), jnp.bfloat16)
        ],
        cost_estimate=estimate(1.7),
        compiler_params=pltpu.CompilerParams(vmem_limit_bytes=VMEM_LIMIT),
        name="step",
    )(info, cols, *args)


def gram_kernel(pairs, info, *refs):
    *powers, mine, theirs, block, held = refs
    columns = mine.shape[1]
    half = columns // 2
    for j, power in enumerate(powers):
        high, low = split(power[...].reshape(-1, columns))
        held[j, :, :columns] = high
        held[j, :, columns:] = low
    for place, (i, j) in enumerate(pairs):
        acc = lax.dot_general(
            held[i], held[j], (((0,), (0,)), ((), ())), preferred_element_type=jnp.float32
        )
        acc = acc[:, :columns] + acc[:, columns:]
        block[place] = acc[:columns] + acc[columns:]
        for core, out in ((info[0], mine), (1 - info[0], theirs)):
            rows = pl.ds(pl.multiple_of(core * half, half), half)
            out[place * half : (place + 1) * half, :] = block[place, rows, :]
    used = len(pairs) * half
    if used < mine.shape[0]:
        for out in (mine, theirs):
            out[used:, :] = jnp.zeros((mine.shape[0] - used, columns), jnp.float32)


def gram_blocks(powers, pairs, info, count):
    columns = powers[0].shape[-1]
    rows = powers[0].size // columns
    whole = pl.BlockSpec(memory_space=pltpu.VMEM)
    tall = share(len(pairs), columns, count) * count
    return pl.pallas_call(
        functools.partial(gram_kernel, pairs),
        in_specs=[pl.BlockSpec(memory_space=pltpu.SMEM)] + [whole] * len(powers),
        out_specs=[whole] * 2,
        out_shape=[jax.ShapeDtypeStruct((tall, columns), jnp.float32)] * 2,
        scratch_shapes=[
            pltpu.VMEM((len(pairs), columns, columns), jnp.float32),
            pltpu.VMEM((len(powers), rows, 2 * columns), jnp.bfloat16),
        ],
        cost_estimate=estimate(1.4),
        compiler_params=pltpu.CompilerParams(vmem_limit_bytes=VMEM_LIMIT),
        name="gram",
    )(info, *powers)


def share(blocks, columns, count):
    return -(-blocks * (columns // 2) // count)


def factor(block):
    size = block.shape[0]
    tall = 8
    tiles = size // tall
    lanes = lax.broadcasted_iota(jnp.int32, (tall, size), 1)
    sub = lax.broadcasted_iota(jnp.int32, (tall, size), 0)
    work = [block[tall * t : tall * (t + 1)] for t in range(tiles)]
    uppers, inverses = [], []

    def spread(x, row):
        return jnp.broadcast_to(x[row : row + 1], (tall, size))

    def lane(x, at):
        return jnp.broadcast_to(x[:, at : at + 1], (tall, size))

    corner = [lane(work[0], c) for c in range(tall)]
    for p in range(tiles):
        at = tall * p
        below = range(p + 1, tiles)
        cols = [[lane(work[t], at + c) for t in below] for c in range(tall)]
        ahead = [lane(work[p + 1], at + tall + d) for d in range(tall)] if p + 1 < tiles else []
        passed = lanes < at + tall
        upper = work[p]
        inverse = jnp.where(lanes == sub + at, 1.0, jnp.where(lanes < at, work[p], 0.0))
        for t in below:
            work[t] = jnp.where(passed & (lanes >= at), 0.0, work[t])
        scales, tops, lows = [], [], []
        for c in range(tall):
            scale = lax.rsqrt(spread(corner[c], c))
            weights = [spread(corner[d], c) * scale for d in range(c + 1, tall)]
            top = jnp.where(sub > c, corner[c], 0.0) * scale
            low = [x * scale for x in cols[c]]
            for d in range(c + 1, tall):
                weight = weights[d - c - 1]
                corner[d] = corner[d] - top * weight
                cols[d] = [x - m * weight for x, m in zip(cols[d], low)]
            if low:
                ahead = [x - low[0] * spread(low[0], d) for d, x in enumerate(ahead)]
            scales.append(scale)
            tops.append(top)
            lows.append(low)
        for c in range(tall):
            row_upper = spread(upper, c) * scales[c]
            row_inverse = spread(inverse, c) * scales[c]
            upper = jnp.where(sub == c, row_upper, upper - tops[c] * row_upper)
            inverse = jnp.where(sub == c, row_inverse, inverse - tops[c] * row_inverse)
            row = jnp.where(passed, row_inverse, row_upper)
            for t, m in zip(below, lows[c]):
                work[t] = work[t] - m * row
        uppers.append(jnp.where(lanes >= sub + at, upper, 0.0))
        inverses.append(inverse)
        corner = ahead
    return jnp.concatenate(uppers, axis=0), jnp.concatenate(inverses, axis=0)


def dot(a, b, right=0):
    (a_high, a_low), (b_high, b_low) = split(a), split(b)

    def product(x, y):
        return lax.dot_general(
            x, y, (((1,), (right,)), ((), ())), preferred_element_type=jnp.float32
        )

    return product(a_high, b_high) + (product(a_high, b_low) + product(a_low, b_high))


def column_kernel(place, first, scale, info, own, other, *refs):
    *refs, upper_out, inverse_out, gram = refs
    size = gram.shape[0]
    half = size // 2
    at = place * size
    for core, source in ((info[0], own), (1 - info[0], other)):
        rows = pl.ds(pl.multiple_of(core * half, half), half)
        for j in range(place + 1):
            gram[rows, j * size : (j + 1) * size] = source[(first + j) * half : (first + j + 1) * half, :]
    corner = gram[:, at:]
    if place:
        known, upper_known = refs
        left = dot(gram[:, :at], known[...], 1)
        corner = corner - dot(left, left, 1)
        carried = dot(left, known[...])
    upper, inverse = factor(corner)
    if place:
        inverse_out[at:, :at] = -dot(inverse, carried)
        inverse_out[:at, :at] = known[...]
        inverse_out[:at, at:] = jnp.zeros((at, size), jnp.float32)
        upper_out[:at, :at] = upper_known[...] * scale
        upper_out[at:, :at] = jnp.zeros((size, at), jnp.float32)
        upper_out[:at, at:] = left.T * scale
    inverse_out[at:, at:] = inverse
    upper_out[at:, at:] = upper * scale


def column(place, first, info, own, other, before, scale=1.0):
    whole = pl.BlockSpec(memory_space=pltpu.VMEM)
    size = own.shape[1]
    args = [own, other, *before]
    square = jax.ShapeDtypeStruct(((place + 1) * size,) * 2, jnp.float32)
    return pl.pallas_call(
        functools.partial(column_kernel, place, first, scale),
        in_specs=[pl.BlockSpec(memory_space=pltpu.SMEM)] + [whole] * len(args),
        out_specs=[whole, whole],
        out_shape=[square, square],
        scratch_shapes=[pltpu.VMEM((size, (place + 1) * size), jnp.float32)],
        compiler_params=pltpu.CompilerParams(vmem_limit_bytes=VMEM_LIMIT),
        cost_estimate=estimate(4.0),
        name="column",
    )(info, *args)


def basis_kernel(scale, count, *refs):
    *powers, inverse, out, high, low = refs
    columns = powers[0].shape[-1]

    @pl.when(pl.program_id(0) == 0)
    def _():
        high[...], low[...] = split(inverse[...] * scale)

    pairs = [split(p[...].reshape(-1, columns)) for p in powers]
    wide = 2 * columns
    for start in range(0, count * columns, wide):
        stop = min(start + wide, count * columns)
        left_high = jnp.concatenate([p[0] for p in pairs[: stop // columns]], axis=1)
        left_low = jnp.concatenate([p[1] for p in pairs[: stop // columns]], axis=1)
        acc = None
        for left, right in ((left_high, high), (left_low, high), (left_high, low)):
            term = lax.dot_general(
                left,
                right[start:stop, :stop],
                (((1,), (1,)), ((), ())),
                preferred_element_type=jnp.float32,
            )
            acc = term if acc is None else acc + term
        out[:, :, :, start:stop] = acc.astype(jnp.bfloat16).reshape(out.shape[:3] + (stop - start,))


def basis_of(powers, inverse, scale):
    layers, cross_local, size, columns = powers[0].shape
    count = len(powers)
    full = count * columns
    return pl.pallas_call(
        functools.partial(basis_kernel, scale, count),
        grid=(layers,),
        in_specs=[pl.BlockSpec((1, cross_local, size, columns), lambda i: (i, 0, 0, 0))] * count
        + [pl.BlockSpec(inverse.shape, lambda i: (0, 0))],
        out_specs=pl.BlockSpec((1, cross_local, size, full), lambda i: (i, 0, 0, 0)),
        out_shape=jax.ShapeDtypeStruct((layers, cross_local, size, full), jnp.bfloat16),
        scratch_shapes=[pltpu.VMEM((full, full), jnp.bfloat16)] * 2,
        compiler_params=pltpu.CompilerParams(vmem_limit_bytes=VMEM_LIMIT),
        cost_estimate=estimate(3.0),
        name="basis",
    )(*powers, inverse)


def local(sources, couplings, block_cols, lead_sites, lead_sigma):
    layers, cross_local, size, columns = sources.shape
    cross_count = lax.axis_size("cross")
    count = lax.axis_size("trans")
    place = lax.axis_index("trans")
    even = 1 - place % 2
    info = jnp.stack([lax.axis_index("cross"), place == 0, place == count - 1, even])
    info = info.astype(jnp.int32)
    packed = pack(couplings, lead_sites, lead_sigma, info)
    scale_rows = math.sqrt(count * layers * cross_local * cross_count * size)

    near = [(i, i ^ 1) for i in range(count) if i ^ 1 < count]
    far = [(i, j) for i in range(count) for j in (i - 1 + 2 * (i % 2),) if 0 <= j < count]

    def swap(x):
        return lax.ppermute(x, "cross", [(0, 1), (1, 0)])

    def exchange(x):
        return lax.all_to_all(x, "trans", 0, 0, tiled=True)

    def double(x, reach, work=None):
        other = lax.ppermute(x, "trans", [(i, i ^ reach) for i in range(count)])
        return x + (other if work is None else lax.optimization_barrier((other, work))[0])

    early = tuple((i, j) for i in range(S) for j in range(i + 1))
    powers = [sources]
    near_layer = lax.dynamic_slice_in_dim(sources, even * (layers - 1), 1)
    far_layer = lax.dynamic_slice_in_dim(sources, (1 - even) * (layers - 1), 1)
    for k in range(S):
        field = powers[k]
        near_edge = lax.ppermute(near_layer, "trans", near)
        far_edge = lax.ppermute(far_layer, "trans", far)
        other = swap(field)
        if k == 0:
            far_edge, near_edge, packed = lax.optimization_barrier((far_edge, near_edge, packed))
        if k == S - 1:
            mine, theirs = gram_blocks(powers, early, info, count)
            theirs, _, _ = lax.optimization_barrier((swap(theirs), near_edge, far_edge))
            parts = exchange((mine + theirs).reshape(count, -1, columns))
        edges = (near_edge, swap(near_edge), far_edge, swap(far_edge))
        before = powers[k - 1] if k else None
        got = step(packed, block_cols, info, field, other, edges, before, k == S - 1)
        powers.append(got[0])
        if k < S - 1:
            near_layer, far_layer = got[1:]
    mine, theirs = gram_blocks(powers, tuple((S, j) for j in range(S + 1)), info, count)
    last = mine + swap(theirs)
    last, parts = lax.optimization_barrier((last, parts))
    summed = jnp.sum(parts, axis=0, keepdims=True)
    known = exchange(jnp.broadcast_to(summed, parts.shape))
    last = double(last, 1)
    known, _ = lax.optimization_barrier((known, last))
    known = known.reshape(-1, columns)
    known_other = swap(known)
    first = column(0, 0, info, known, known_other, ())
    second = column(1, 1, info, known, known_other, first[::-1])
    third = column(2, 3, info, known, known_other, second[::-1])
    reach = 2
    while reach < count:
        work = third if 2 * reach == count else first if 4 * reach == count else None
        last = double(last, reach, work)
        reach *= 2
    r_factor, inverse = column(3, 0, info, last, swap(last), third[::-1], 1.0 / scale_rows)
    return basis_of(powers, inverse, scale_rows), r_factor


def solution(mesh):
    return jax.shard_map(
        local,
        mesh=mesh,
        in_specs=(
            P(("energy", "trans"), "cross", None, None),
            P(("energy", "trans"), "cross", None, None, None),
            P("trans", "cross", None),
            P(),
            P("energy", None, None),
        ),
        out_specs=(P(("energy", "trans"), "cross", None, None), P("energy", None)),
        check_vma=False,
    )
```

```python
import functools
import math

import jax
import jax.numpy as jnp
from jax import lax
from jax.experimental import pallas as pl
from jax.experimental.pallas import tpu as pltpu
from jax.sharding import PartitionSpec as P

S = 3
center_shift = 2.0
half_range = 1.6
VMEM_LIMIT = 16 * 1024 * 1024


def estimate(us):
    return pl.CostEstimate(flops=int(us * 1.15e9), bytes_accessed=0, transcendentals=0)


def split(x):
    high = x.astype(jnp.bfloat16)
    low = (x - high.astype(jnp.float32)).astype(jnp.bfloat16)
    return high, low


def pack_kernel(info, sites, held, leads, out):
    layers, cross_local, slots, size, _ = held.shape
    contacts = leads.shape[0]
    for layer in range(layers):
        for q in range(cross_local):
            place = info[0] * cross_local + q
            lead = jnp.zeros((size, size), jnp.float32)
            for k in range(contacts):
                end, flag = (0, info[1]) if k < contacts // 2 else (layers - 1, info[2])
                if layer == end:
                    here = jnp.logical_and(flag == 1, sites[k] == place)
                    lead = lead - leads[k] * jnp.where(here, 1.0, 0.0)
            blocks = [held[layer, q, j] for j in range(slots)] + [lead]
            row = jnp.concatenate(
                [jnp.concatenate(blocks[i : i + 2], axis=1) for i in range(0, slots + 1, 2)],
                axis=1,
            )
            high, low = split(row)
            out[layer * cross_local + q, :size] = high
            out[layer * cross_local + q, size:] = low


def pack(couplings, lead_sites, lead_sigma, info):
    layers, cross_local, slots, size, _ = couplings.shape
    scalar = pl.BlockSpec(memory_space=pltpu.SMEM)
    whole = pl.BlockSpec(memory_space=pltpu.VMEM)
    return pl.pallas_call(
        pack_kernel,
        in_specs=[scalar, scalar, whole, whole],
        out_specs=whole,
        out_shape=jax.ShapeDtypeStruct(
            (layers * cross_local, 2 * size, (slots + 1) * size), jnp.bfloat16
        ),
        compiler_params=pltpu.CompilerParams(vmem_limit_bytes=VMEM_LIMIT),
        cost_estimate=estimate(2.5),
        name="pack",
    )(info, lead_sites, couplings, lead_sigma)


def step_kernel(first, last, slots, info, cols, packed, own, other, *refs):
    edges, refs = refs[:4], refs[4:]
    before, refs = (None, refs) if first else (refs[0], refs[1:])
    out, field = refs[0], refs[-1]
    layers, cross_local, size, columns = own.shape
    total = 2 * cross_local
    mine = info[0] * cross_local
    theirs = (1 - info[0]) * cross_local

    def put(place, x):
        high, low = split(x)
        field[place, :, :columns] = high
        field[place, :, columns:] = low

    for layer in range(layers):
        for q in range(cross_local):
            put((layer + 1) * total + mine + q, own[layer, q])
            put((layer + 1) * total + theirs + q, other[layer, q])
    even = info[3]
    for pair, place in enumerate((even, 1 - even)):
        for q in range(cross_local):
            put(place * (layers + 1) * total + mine + q, edges[2 * pair][0, q])
            put(place * (layers + 1) * total + theirs + q, edges[2 * pair + 1][0, q])
    for layer in range(layers):
        for q in range(cross_local):
            row = layer * cross_local + q
            places = [cols[layer, q, j] for j in range(slots)] + [total + mine + q]
            picked = jnp.concatenate([field[layer * total + c] for c in places], axis=0)
            acc = jnp.dot(packed[row], picked, preferred_element_type=jnp.float32)
            acc = acc[:, :columns] + acc[:, columns:]
            applied = acc[:size] + acc[size:]
            value = (applied - center_shift * own[layer, q]) * (1.0 / half_range)
            if not first:
                value = 2.0 * value - before[layer, q]
            out[layer, q] = value
    if not last:
        refs[1][0] = out[even * (layers - 1)]
        refs[2][0] = out[(1 - even) * (layers - 1)]


def step(packed, cols, info, own, other, edges, before, last):
    layers, cross_local, size, columns = own.shape
    rows, _, depth = packed.shape
    whole = pl.BlockSpec(memory_space=pltpu.VMEM)
    scalar = pl.BlockSpec(memory_space=pltpu.SMEM)
    args = [packed, own, other, *edges] + ([] if before is None else [before])
    edge = jax.ShapeDtypeStruct((1,) + own.shape[1:], jnp.float32)
    shapes = [jax.ShapeDtypeStruct(own.shape, jnp.float32)] + ([] if last else [edge, edge])
    return pl.pallas_call(
        functools.partial(step_kernel, before is None, last, cols.shape[2]),
        in_specs=[scalar, scalar] + [whole] * len(args),
        out_specs=[whole] * len(shapes),
        out_shape=shapes,
        scratch_shapes=[
            pltpu.VMEM(((layers + 2) * 2 * cross_local, size, 2 * columns), jnp.bfloat16)
        ],
        cost_estimate=estimate(1.7),
        compiler_params=pltpu.CompilerParams(vmem_limit_bytes=VMEM_LIMIT),
        name="step",
    )(info, cols, *args)


def gram_kernel(pairs, info, *refs):
    *powers, mine, theirs, block, held = refs
    columns = mine.shape[1]
    half = columns // 2
    for j, power in enumerate(powers):
        high, low = split(power[...].reshape(-1, columns))
        held[j, :, :columns] = high
        held[j, :, columns:] = low
    for place, (i, j) in enumerate(pairs):
        acc = lax.dot_general(
            held[i], held[j], (((0,), (0,)), ((), ())), preferred_element_type=jnp.float32
        )
        acc = acc[:, :columns] + acc[:, columns:]
        block[place] = acc[:columns] + acc[columns:]
        for core, out in ((info[0], mine), (1 - info[0], theirs)):
            rows = pl.ds(pl.multiple_of(core * half, half), half)
            out[place * half : (place + 1) * half, :] = block[place, rows, :]
    used = len(pairs) * half
    if used < mine.shape[0]:
        for out in (mine, theirs):
            out[used:, :] = jnp.zeros((mine.shape[0] - used, columns), jnp.float32)


def gram_blocks(powers, pairs, info, count):
    columns = powers[0].shape[-1]
    rows = powers[0].size // columns
    whole = pl.BlockSpec(memory_space=pltpu.VMEM)
    tall = share(len(pairs), columns, count) * count
    return pl.pallas_call(
        functools.partial(gram_kernel, pairs),
        in_specs=[pl.BlockSpec(memory_space=pltpu.SMEM)] + [whole] * len(powers),
        out_specs=[whole] * 2,
        out_shape=[jax.ShapeDtypeStruct((tall, columns), jnp.float32)] * 2,
        scratch_shapes=[
            pltpu.VMEM((len(pairs), columns, columns), jnp.float32),
            pltpu.VMEM((len(powers), rows, 2 * columns), jnp.bfloat16),
        ],
        cost_estimate=estimate(1.4),
        compiler_params=pltpu.CompilerParams(vmem_limit_bytes=VMEM_LIMIT),
        name="gram",
    )(info, *powers)


def share(blocks, columns, count):
    return -(-blocks * (columns // 2) // count)


def factor(block):
    size = block.shape[0]
    tall = 8
    tiles = size // tall
    lanes = lax.broadcasted_iota(jnp.int32, (tall, size), 1)
    sub = lax.broadcasted_iota(jnp.int32, (tall, size), 0)
    work = [block[tall * t : tall * (t + 1)] for t in range(tiles)]
    uppers, inverses = [], []

    def spread(x, row):
        return jnp.broadcast_to(x[row : row + 1], (tall, size))

    def lane(x, at):
        return jnp.broadcast_to(x[:, at : at + 1], (tall, size))

    corner = [lane(work[0], c) for c in range(tall)]
    for p in range(tiles):
        at = tall * p
        below = range(p + 1, tiles)
        cols = [[lane(work[t], at + c) for t in below] for c in range(tall)]
        ahead = [lane(work[p + 1], at + tall + d) for d in range(tall)] if p + 1 < tiles else []
        passed = lanes < at + tall
        upper = work[p]
        inverse = jnp.where(lanes == sub + at, 1.0, jnp.where(lanes < at, work[p], 0.0))
        for t in below:
            work[t] = jnp.where(passed & (lanes >= at), 0.0, work[t])
        scales, tops, lows = [], [], []
        for c in range(tall):
            scale = lax.rsqrt(spread(corner[c], c))
            weights = [spread(corner[d], c) * scale for d in range(c + 1, tall)]
            top = jnp.where(sub > c, corner[c], 0.0) * scale
            low = [x * scale for x in cols[c]]
            for d in range(c + 1, tall):
                weight = weights[d - c - 1]
                corner[d] = corner[d] - top * weight
                cols[d] = [x - m * weight for x, m in zip(cols[d], low)]
            if low:
                ahead = [x - low[0] * spread(low[0], d) for d, x in enumerate(ahead)]
            scales.append(scale)
            tops.append(top)
            lows.append(low)
        for c in range(tall):
            row_upper = spread(upper, c) * scales[c]
            row_inverse = spread(inverse, c) * scales[c]
            upper = jnp.where(sub == c, row_upper, upper - tops[c] * row_upper)
            inverse = jnp.where(sub == c, row_inverse, inverse - tops[c] * row_inverse)
            row = jnp.where(passed, row_inverse, row_upper)
            for t, m in zip(below, lows[c]):
                work[t] = work[t] - m * row
        uppers.append(jnp.where(lanes >= sub + at, upper, 0.0))
        inverses.append(inverse)
        corner = ahead
    return jnp.concatenate(uppers, axis=0), jnp.concatenate(inverses, axis=0)


def dot(a, b, right=0):
    (a_high, a_low), (b_high, b_low) = split(a), split(b)

    def product(x, y):
        return lax.dot_general(
            x, y, (((1,), (right,)), ((), ())), preferred_element_type=jnp.float32
        )

    return product(a_high, b_high) + (product(a_high, b_low) + product(a_low, b_high))


def column_kernel(place, first, scale, info, own, other, *refs):
    *refs, upper_out, inverse_out, gram = refs
    size = gram.shape[0]
    half = size // 2
    at = place * size
    for core, source in ((info[0], own), (1 - info[0], other)):
        rows = pl.ds(pl.multiple_of(core * half, half), half)
        for j in range(place + 1):
            gram[rows, j * size : (j + 1) * size] = source[(first + j) * half : (first + j + 1) * half, :]
    corner = gram[:, at:]
    if place:
        known, upper_known = refs
        left = dot(gram[:, :at], known[...], 1)
        corner = corner - dot(left, left, 1)
        carried = dot(left, known[...])
    upper, inverse = factor(corner)
    if place:
        inverse_out[at:, :at] = -dot(inverse, carried)
        inverse_out[:at, :at] = known[...]
        inverse_out[:at, at:] = jnp.zeros((at, size), jnp.float32)
        upper_out[:at, :at] = upper_known[...] * scale
        upper_out[at:, :at] = jnp.zeros((size, at), jnp.float32)
        upper_out[:at, at:] = left.T * scale
    inverse_out[at:, at:] = inverse
    upper_out[at:, at:] = upper * scale


def column(place, first, info, own, other, before, scale=1.0):
    whole = pl.BlockSpec(memory_space=pltpu.VMEM)
    size = own.shape[1]
    args = [own, other, *before]
    square = jax.ShapeDtypeStruct(((place + 1) * size,) * 2, jnp.float32)
    return pl.pallas_call(
        functools.partial(column_kernel, place, first, scale),
        in_specs=[pl.BlockSpec(memory_space=pltpu.SMEM)] + [whole] * len(args),
        out_specs=[whole, whole],
        out_shape=[square, square],
        scratch_shapes=[pltpu.VMEM((size, (place + 1) * size), jnp.float32)],
        compiler_params=pltpu.CompilerParams(vmem_limit_bytes=VMEM_LIMIT),
        cost_estimate=estimate(4.0),
        name="column",
    )(info, *args)


def basis_kernel(scale, count, *refs):
    *powers, inverse, upper, out, upper_out, high, low = refs
    columns = powers[0].shape[-1]
    upper_out[...] = upper[...]

    @pl.when(pl.program_id(0) == 0)
    def _():
        high[...], low[...] = split(inverse[...] * scale)

    pairs = [split(p[...].reshape(-1, columns)) for p in powers]
    wide = 2 * columns
    for start in range(0, count * columns, wide):
        stop = min(start + wide, count * columns)
        left_high = jnp.concatenate([p[0] for p in pairs[: stop // columns]], axis=1)
        left_low = jnp.concatenate([p[1] for p in pairs[: stop // columns]], axis=1)
        acc = None
        for left, right in ((left_high, high), (left_low, high), (left_high, low)):
            term = lax.dot_general(
                left,
                right[start:stop, :stop],
                (((1,), (1,)), ((), ())),
                preferred_element_type=jnp.float32,
            )
            acc = term if acc is None else acc + term
        out[:, :, :, start:stop] = acc.astype(jnp.bfloat16).reshape(out.shape[:3] + (stop - start,))


def basis_of(powers, inverse, upper, scale):
    layers, cross_local, size, columns = powers[0].shape
    count = len(powers)
    full = count * columns
    part = pl.BlockSpec((full // layers, full), lambda i: (i, 0))
    return pl.pallas_call(
        functools.partial(basis_kernel, scale, count),
        grid=(layers,),
        in_specs=[pl.BlockSpec((1, cross_local, size, columns), lambda i: (i, 0, 0, 0))] * count
        + [pl.BlockSpec(inverse.shape, lambda i: (0, 0)), part],
        out_specs=[pl.BlockSpec((1, cross_local, size, full), lambda i: (i, 0, 0, 0)), part],
        out_shape=[
            jax.ShapeDtypeStruct((layers, cross_local, size, full), jnp.bfloat16),
            jax.ShapeDtypeStruct(upper.shape, jnp.float32),
        ],
        scratch_shapes=[pltpu.VMEM((full, full), jnp.bfloat16)] * 2,
        compiler_params=pltpu.CompilerParams(vmem_limit_bytes=VMEM_LIMIT),
        cost_estimate=estimate(3.0),
        name="basis",
    )(*powers, inverse, upper)


def local(sources, couplings, block_cols, lead_sites, lead_sigma):
    layers, cross_local, size, columns = sources.shape
    cross_count = lax.axis_size("cross")
    count = lax.axis_size("trans")
    place = lax.axis_index("trans")
    even = 1 - place % 2
    info = jnp.stack([lax.axis_index("cross"), place == 0, place == count - 1, even])
    info = info.astype(jnp.int32)
    packed = pack(couplings, lead_sites, lead_sigma, info)
    scale_rows = math.sqrt(count * layers * cross_local * cross_count * size)

    near = [(i, i ^ 1) for i in range(count) if i ^ 1 < count]
    far = [(i, j) for i in range(count) for j in (i - 1 + 2 * (i % 2),) if 0 <= j < count]

    def swap(x):
        return lax.ppermute(x, "cross", [(0, 1), (1, 0)])

    def exchange(x):
        return lax.all_to_all(x, "trans", 0, 0, tiled=True)

    def double(x, reach, work=None):
        other = lax.ppermute(x, "trans", [(i, i ^ reach) for i in range(count)])
        return x + (other if work is None else lax.optimization_barrier((other, work))[0])

    early = tuple((i, j) for i in range(S) for j in range(i + 1))
    powers = [sources]
    near_layer = lax.dynamic_slice_in_dim(sources, even * (layers - 1), 1)
    far_layer = lax.dynamic_slice_in_dim(sources, (1 - even) * (layers - 1), 1)
    for k in range(S):
        field = powers[k]
        near_edge = lax.ppermute(near_layer, "trans", near)
        far_edge = lax.ppermute(far_layer, "trans", far)
        other = swap(field)
        if k == 0:
            far_edge, near_edge, packed = lax.optimization_barrier((far_edge, near_edge, packed))
        if k == S - 1:
            mine, theirs = gram_blocks(powers, early, info, count)
            theirs, _, _ = lax.optimization_barrier((swap(theirs), near_edge, far_edge))
            parts = exchange((mine + theirs).reshape(count, -1, columns))
        edges = (near_edge, swap(near_edge), far_edge, swap(far_edge))
        before = powers[k - 1] if k else None
        got = step(packed, block_cols, info, field, other, edges, before, k == S - 1)
        powers.append(got[0])
        if k < S - 1:
            near_layer, far_layer = got[1:]
    mine, theirs = gram_blocks(powers, tuple((S, j) for j in range(S + 1)), info, count)
    last = mine + swap(theirs)
    last, parts = lax.optimization_barrier((last, parts))
    summed = jnp.sum(parts, axis=0, keepdims=True)
    known = exchange(jnp.broadcast_to(summed, parts.shape))
    last = double(last, 1)
    known, _ = lax.optimization_barrier((known, last))
    known = known.reshape(-1, columns)
    known_other = swap(known)
    first = column(0, 0, info, known, known_other, ())
    second = column(1, 1, info, known, known_other, first[::-1])
    third = column(2, 3, info, known, known_other, second[::-1])
    reach = 2
    while reach < count:
        work = third if 2 * reach == count else first if 4 * reach == count else None
        last = double(last, reach, work)
        reach *= 2
    r_factor, inverse = column(3, 0, info, last, swap(last), third[::-1], 1.0 / scale_rows)
    return tuple(basis_of(powers, inverse, r_factor, scale_rows))


def solution(mesh):
    return jax.shard_map(
        local,
        mesh=mesh,
        in_specs=(
            P(("energy", "trans"), "cross", None, None),
            P(("energy", "trans"), "cross", None, None, None),
            P("trans", "cross", None),
            P(),
            P("energy", None, None),
        ),
        out_specs=(P(("energy", "trans"), "cross", None, None), P("energy", None)),
        check_vma=False,
    )
```

```python
import functools
import math

import jax
import jax.numpy as jnp
from jax import lax
from jax.experimental import pallas as pl
from jax.experimental.pallas import tpu as pltpu
from jax.sharding import PartitionSpec as P

S = 3
center_shift = 2.0
half_range = 1.6
VMEM_LIMIT = 16 * 1024 * 1024


def estimate(us):
    return pl.CostEstimate(flops=int(us * 1.15e9), bytes_accessed=0, transcendentals=0)


def split(x):
    high = x.astype(jnp.bfloat16)
    low = (x - high.astype(jnp.float32)).astype(jnp.bfloat16)
    return high, low


def pack_kernel(info, held, leads, out):
    layers, cross_local, slots, size, _ = held.shape
    contacts = leads.shape[0]
    for layer in range(layers):
        for q in range(cross_local):
            place = info[0] * cross_local + q
            lead = jnp.zeros((size, size), jnp.float32)
            for k in range(contacts):
                end, flag = (0, info[1]) if k < contacts // 2 else (layers - 1, info[2])
                if layer == end:
                    here = jnp.logical_and(flag == 1, info[4 + k] == place)
                    lead = lead - leads[k] * jnp.where(here, 1.0, 0.0)
            blocks = [held[layer, q, j] for j in range(slots)] + [lead]
            row = jnp.concatenate(
                [jnp.concatenate(blocks[i : i + 2], axis=1) for i in range(0, slots + 1, 2)],
                axis=1,
            )
            high, low = split(row)
            out[layer * cross_local + q, :size] = high
            out[layer * cross_local + q, size:] = low


def pack(couplings, lead_sigma, info):
    layers, cross_local, slots, size, _ = couplings.shape
    scalar = pl.BlockSpec(memory_space=pltpu.SMEM)
    whole = pl.BlockSpec(memory_space=pltpu.VMEM)
    return pl.pallas_call(
        pack_kernel,
        in_specs=[scalar, whole, whole],
        out_specs=whole,
        out_shape=jax.ShapeDtypeStruct(
            (layers * cross_local, 2 * size, (slots + 1) * size), jnp.bfloat16
        ),
        compiler_params=pltpu.CompilerParams(vmem_limit_bytes=VMEM_LIMIT),
        cost_estimate=estimate(2.5),
        name="pack",
    )(info, couplings, lead_sigma)


def step_kernel(first, last, slots, info, cols, packed, own, other, *refs):
    edges, refs = refs[:4], refs[4:]
    before, refs = (None, refs) if first else (refs[0], refs[1:])
    out, field = refs[0], refs[-1]
    layers, cross_local, size, columns = own.shape
    total = 2 * cross_local
    mine = info[0] * cross_local
    theirs = (1 - info[0]) * cross_local

    def put(place, x):
        high, low = split(x)
        field[place, :, :columns] = high
        field[place, :, columns:] = low

    for layer in range(layers):
        for q in range(cross_local):
            put((layer + 1) * total + mine + q, own[layer, q])
            put((layer + 1) * total + theirs + q, other[layer, q])
    even = info[3]
    for pair, place in enumerate((even, 1 - even)):
        for q in range(cross_local):
            put(place * (layers + 1) * total + mine + q, edges[2 * pair][0, q])
            put(place * (layers + 1) * total + theirs + q, edges[2 * pair + 1][0, q])
    for layer in range(layers):
        for q in range(cross_local):
            row = layer * cross_local + q
            places = [cols[layer, q, j] for j in range(slots)] + [total + mine + q]
            picked = jnp.concatenate([field[layer * total + c] for c in places], axis=0)
            acc = jnp.dot(packed[row], picked, preferred_element_type=jnp.float32)
            acc = acc[:, :columns] + acc[:, columns:]
            applied = acc[:size] + acc[size:]
            value = (applied - center_shift * own[layer, q]) * (1.0 / half_range)
            if not first:
                value = 2.0 * value - before[layer, q]
            out[layer, q] = value
    if not last:
        refs[1][0] = out[even * (layers - 1)]
        refs[2][0] = out[(1 - even) * (layers - 1)]


def step(packed, cols, info, own, other, edges, before, last):
    layers, cross_local, size, columns = own.shape
    rows, _, depth = packed.shape
    whole = pl.BlockSpec(memory_space=pltpu.VMEM)
    scalar = pl.BlockSpec(memory_space=pltpu.SMEM)
    args = [packed, own, other, *edges] + ([] if before is None else [before])
    edge = jax.ShapeDtypeStruct((1,) + own.shape[1:], jnp.float32)
    shapes = [jax.ShapeDtypeStruct(own.shape, jnp.float32)] + ([] if last else [edge, edge])
    return pl.pallas_call(
        functools.partial(step_kernel, before is None, last, cols.shape[2]),
        in_specs=[scalar, scalar] + [whole] * len(args),
        out_specs=[whole] * len(shapes),
        out_shape=shapes,
        scratch_shapes=[
            pltpu.VMEM(((layers + 2) * 2 * cross_local, size, 2 * columns), jnp.bfloat16)
        ],
        cost_estimate=estimate(1.7),
        compiler_params=pltpu.CompilerParams(vmem_limit_bytes=VMEM_LIMIT),
        name="step",
    )(info, cols, *args)


def gram_kernel(pairs, info, *refs):
    *powers, mine, theirs, block, held = refs
    columns = mine.shape[1]
    half = columns // 2
    for j, power in enumerate(powers):
        high, low = split(power[...].reshape(-1, columns))
        held[j, :, :columns] = high
        held[j, :, columns:] = low
    for place, (i, j) in enumerate(pairs):
        acc = lax.dot_general(
            held[i], held[j], (((0,), (0,)), ((), ())), preferred_element_type=jnp.float32
        )
        acc = acc[:, :columns] + acc[:, columns:]
        block[place] = acc[:columns] + acc[columns:]
        for core, out in ((info[0], mine), (1 - info[0], theirs)):
            rows = pl.ds(pl.multiple_of(core * half, half), half)
            out[place * half : (place + 1) * half, :] = block[place, rows, :]
    used = len(pairs) * half
    if used < mine.shape[0]:
        for out in (mine, theirs):
            out[used:, :] = jnp.zeros((mine.shape[0] - used, columns), jnp.float32)


def gram_blocks(powers, pairs, info, count):
    columns = powers[0].shape[-1]
    rows = powers[0].size // columns
    whole = pl.BlockSpec(memory_space=pltpu.VMEM)
    tall = share(len(pairs), columns, count) * count
    return pl.pallas_call(
        functools.partial(gram_kernel, pairs),
        in_specs=[pl.BlockSpec(memory_space=pltpu.SMEM)] + [whole] * len(powers),
        out_specs=[whole] * 2,
        out_shape=[jax.ShapeDtypeStruct((tall, columns), jnp.float32)] * 2,
        scratch_shapes=[
            pltpu.VMEM((len(pairs), columns, columns), jnp.float32),
            pltpu.VMEM((len(powers), rows, 2 * columns), jnp.bfloat16),
        ],
        cost_estimate=estimate(1.4),
        compiler_params=pltpu.CompilerParams(vmem_limit_bytes=VMEM_LIMIT),
        name="gram",
    )(info, *powers)


def share(blocks, columns, count):
    return -(-blocks * (columns // 2) // count)


def factor(block):
    size = block.shape[0]
    tall = 8
    tiles = size // tall
    lanes = lax.broadcasted_iota(jnp.int32, (tall, size), 1)
    sub = lax.broadcasted_iota(jnp.int32, (tall, size), 0)
    work = [block[tall * t : tall * (t + 1)] for t in range(tiles)]
    uppers, inverses = [], []

    def spread(x, row):
        return jnp.broadcast_to(x[row : row + 1], (tall, size))

    def lane(x, at):
        return jnp.broadcast_to(x[:, at : at + 1], (tall, size))

    corner = [lane(work[0], c) for c in range(tall)]
    for p in range(tiles):
        at = tall * p
        below = range(p + 1, tiles)
        cols = [[lane(work[t], at + c) for t in below] for c in range(tall)]
        ahead = [lane(work[p + 1], at + tall + d) for d in range(tall)] if p + 1 < tiles else []
        passed = lanes < at + tall
        upper = work[p]
        inverse = jnp.where(lanes == sub + at, 1.0, jnp.where(lanes < at, work[p], 0.0))
        for t in below:
            work[t] = jnp.where(passed & (lanes >= at), 0.0, work[t])
        scales, tops, lows = [], [], []
        for c in range(tall):
            scale = lax.rsqrt(spread(corner[c], c))
            weights = [spread(corner[d], c) * scale for d in range(c + 1, tall)]
            top = jnp.where(sub > c, corner[c], 0.0) * scale
            low = [x * scale for x in cols[c]]
            for d in range(c + 1, tall):
                weight = weights[d - c - 1]
                corner[d] = corner[d] - top * weight
                cols[d] = [x - m * weight for x, m in zip(cols[d], low)]
            if low:
                ahead = [x - low[0] * spread(low[0], d) for d, x in enumerate(ahead)]
            scales.append(scale)
            tops.append(top)
            lows.append(low)
        for c in range(tall):
            row_upper = spread(upper, c) * scales[c]
            row_inverse = spread(inverse, c) * scales[c]
            upper = jnp.where(sub == c, row_upper, upper - tops[c] * row_upper)
            inverse = jnp.where(sub == c, row_inverse, inverse - tops[c] * row_inverse)
            row = jnp.where(passed, row_inverse, row_upper)
            for t, m in zip(below, lows[c]):
                work[t] = work[t] - m * row
        uppers.append(jnp.where(lanes >= sub + at, upper, 0.0))
        inverses.append(inverse)
        corner = ahead
    return jnp.concatenate(uppers, axis=0), jnp.concatenate(inverses, axis=0)


def dot(a, b, right=0):
    (a_high, a_low), (b_high, b_low) = split(a), split(b)

    def product(x, y):
        return lax.dot_general(
            x, y, (((1,), (right,)), ((), ())), preferred_element_type=jnp.float32
        )

    return product(a_high, b_high) + (product(a_high, b_low) + product(a_low, b_high))


def column_kernel(place, first, scale, info, own, other, *refs):
    *refs, upper_out, inverse_out, gram = refs
    size = gram.shape[0]
    half = size // 2
    at = place * size
    for core, source in ((info[0], own), (1 - info[0], other)):
        rows = pl.ds(pl.multiple_of(core * half, half), half)
        for j in range(place + 1):
            gram[rows, j * size : (j + 1) * size] = source[(first + j) * half : (first + j + 1) * half, :]
    corner = gram[:, at:]
    if place:
        known, upper_known = refs
        left = dot(gram[:, :at], known[...], 1)
        corner = corner - dot(left, left, 1)
        carried = dot(left, known[...])
    upper, inverse = factor(corner)
    if place:
        inverse_out[at:, :at] = -dot(inverse, carried)
        inverse_out[:at, :at] = known[...]
        inverse_out[:at, at:] = jnp.zeros((at, size), jnp.float32)
        upper_out[:at, :at] = upper_known[...] * scale
        upper_out[at:, :at] = jnp.zeros((size, at), jnp.float32)
        upper_out[:at, at:] = left.T * scale
    inverse_out[at:, at:] = inverse
    upper_out[at:, at:] = upper * scale


def column(place, first, info, own, other, before, scale=1.0):
    whole = pl.BlockSpec(memory_space=pltpu.VMEM)
    size = own.shape[1]
    args = [own, other, *before]
    square = jax.ShapeDtypeStruct(((place + 1) * size,) * 2, jnp.float32)
    return pl.pallas_call(
        functools.partial(column_kernel, place, first, scale),
        in_specs=[pl.BlockSpec(memory_space=pltpu.SMEM)] + [whole] * len(args),
        out_specs=[whole, whole],
        out_shape=[square, square],
        scratch_shapes=[pltpu.VMEM((size, (place + 1) * size), jnp.float32)],
        compiler_params=pltpu.CompilerParams(vmem_limit_bytes=VMEM_LIMIT),
        cost_estimate=estimate(4.0),
        name="column",
    )(info, *args)


def basis_kernel(scale, count, *refs):
    *powers, inverse, upper, out, upper_out, high, low = refs
    columns = powers[0].shape[-1]
    upper_out[...] = upper[...]

    @pl.when(pl.program_id(0) == 0)
    def _():
        high[...], low[...] = split(inverse[...] * scale)

    pairs = [split(p[...].reshape(-1, columns)) for p in powers]
    wide = 2 * columns
    for start in range(0, count * columns, wide):
        stop = min(start + wide, count * columns)
        left_high = jnp.concatenate([p[0] for p in pairs[: stop // columns]], axis=1)
        left_low = jnp.concatenate([p[1] for p in pairs[: stop // columns]], axis=1)
        acc = None
        for left, right in ((left_high, high), (left_low, high), (left_high, low)):
            term = lax.dot_general(
                left,
                right[start:stop, :stop],
                (((1,), (1,)), ((), ())),
                preferred_element_type=jnp.float32,
            )
            acc = term if acc is None else acc + term
        out[:, :, :, start:stop] = acc.astype(jnp.bfloat16).reshape(out.shape[:3] + (stop - start,))


def basis_of(powers, inverse, upper, scale):
    layers, cross_local, size, columns = powers[0].shape
    count = len(powers)
    full = count * columns
    part = pl.BlockSpec((full // layers, full), lambda i: (i, 0))
    return pl.pallas_call(
        functools.partial(basis_kernel, scale, count),
        grid=(layers,),
        in_specs=[pl.BlockSpec((1, cross_local, size, columns), lambda i: (i, 0, 0, 0))] * count
        + [pl.BlockSpec(inverse.shape, lambda i: (0, 0)), part],
        out_specs=[pl.BlockSpec((1, cross_local, size, full), lambda i: (i, 0, 0, 0)), part],
        out_shape=[
            jax.ShapeDtypeStruct((layers, cross_local, size, full), jnp.bfloat16),
            jax.ShapeDtypeStruct(upper.shape, jnp.float32),
        ],
        scratch_shapes=[pltpu.VMEM((full, full), jnp.bfloat16)] * 2,
        compiler_params=pltpu.CompilerParams(vmem_limit_bytes=VMEM_LIMIT),
        cost_estimate=estimate(3.0),
        name="basis",
    )(*powers, inverse, upper)


def local(sources, couplings, block_cols, lead_sites, lead_sigma):
    layers, cross_local, size, columns = sources.shape
    cross_count = lax.axis_size("cross")
    count = lax.axis_size("trans")
    place = lax.axis_index("trans")
    even = 1 - place % 2
    sites = [lead_sites[k] for k in range(lead_sites.shape[0])]
    info = jnp.stack([lax.axis_index("cross"), place == 0, place == count - 1, even, *sites])
    info = info.astype(jnp.int32)
    packed = pack(couplings, lead_sigma, info)
    scale_rows = math.sqrt(count * layers * cross_local * cross_count * size)

    near = [(i, i ^ 1) for i in range(count) if i ^ 1 < count]
    far = [(i, j) for i in range(count) for j in (i - 1 + 2 * (i % 2),) if 0 <= j < count]

    def swap(x):
        return lax.ppermute(x, "cross", [(0, 1), (1, 0)])

    def exchange(x):
        return lax.all_to_all(x, "trans", 0, 0, tiled=True)

    def double(x, reach, work=None):
        other = lax.ppermute(x, "trans", [(i, i ^ reach) for i in range(count)])
        return x + (other if work is None else lax.optimization_barrier((other, work))[0])

    early = tuple((i, j) for i in range(S) for j in range(i + 1))
    powers = [sources]
    near_layer = lax.dynamic_slice_in_dim(sources, even * (layers - 1), 1)
    far_layer = lax.dynamic_slice_in_dim(sources, (1 - even) * (layers - 1), 1)
    for k in range(S):
        field = powers[k]
        near_edge = lax.ppermute(near_layer, "trans", near)
        far_edge = lax.ppermute(far_layer, "trans", far)
        other = swap(field)
        if k == 0:
            far_edge, near_edge, packed = lax.optimization_barrier((far_edge, near_edge, packed))
        if k == S - 1:
            mine, theirs = gram_blocks(powers, early, info, count)
            theirs, _, _ = lax.optimization_barrier((swap(theirs), near_edge, far_edge))
            parts = exchange((mine + theirs).reshape(count, -1, columns))
        edges = (near_edge, swap(near_edge), far_edge, swap(far_edge))
        before = powers[k - 1] if k else None
        got = step(packed, block_cols, info, field, other, edges, before, k == S - 1)
        powers.append(got[0])
        if k < S - 1:
            near_layer, far_layer = got[1:]
    mine, theirs = gram_blocks(powers, tuple((S, j) for j in range(S + 1)), info, count)
    last = mine + swap(theirs)
    last, parts = lax.optimization_barrier((last, parts))
    summed = jnp.sum(parts, axis=0, keepdims=True)
    known = exchange(jnp.broadcast_to(summed, parts.shape))
    last = double(last, 1)
    known, _ = lax.optimization_barrier((known, last))
    known = known.reshape(-1, columns)
    known_other = swap(known)
    first = column(0, 0, info, known, known_other, ())
    second = column(1, 1, info, known, known_other, first[::-1])
    third = column(2, 3, info, known, known_other, second[::-1])
    reach = 2
    while reach < count:
        work = third if 2 * reach == count else first if 4 * reach == count else None
        last = double(last, reach, work)
        reach *= 2
    r_factor, inverse = column(3, 0, info, last, swap(last), third[::-1], 1.0 / scale_rows)
    return tuple(basis_of(powers, inverse, r_factor, scale_rows))


def solution(mesh):
    return jax.shard_map(
        local,
        mesh=mesh,
        in_specs=(
            P(("energy", "trans"), "cross", None, None),
            P(("energy", "trans"), "cross", None, None, None),
            P("trans", "cross", None),
            P(),
            P("energy", None, None),
        ),
        out_specs=(P(("energy", "trans"), "cross", None, None), P("energy", None)),
        check_vma=False,
    )
```
